128 devices in a mesh: row: 8 (over y_lo, x), col: 16 (over z, y_hi, core).
Axes of the slice: x: 4, y: 4 (y_hi: 2, y_lo: 2; y = y_hi * 2 + y_lo), z: 4, core: 2. Of those that a mesh axis runs over, the one named last changes fastest.
Arguments:
- front_init: float32 [4, 8, 2, 16, 512, 512], P(None, 'row', None, 'col'), as said below
- child_tiles: bfloat16 [8, 16, 8, 512, 512], P('row', 'col'), may hold values from -0.29882812 to 0.29882812
- child_map: int32 [8, 16, 8, 2], replicated, may hold values from 0 to 31, as said below
- child_counts: int32 [8, 16], replicated, may hold values from 5 to 8
- child_extent: int32 [8, 16, 8], replicated, may hold values from 128 to 512
Outputs:
- schur: float32 [4, 8, 2, 16, 512, 512], P(None, 'row', None, 'col')
- panel: float32 [4, 8, 512, 512], P(None, 'row')
The draws below stay inside these ranges and needn't reach their ends.
Inputs may be any that keep to these rules, and one draw needn't show every extreme that they name: child_map[r, c, s, 0] is congruent to r modulo 8; the live slots of one grid position name tile columns that are all different modulo 16; in every process row some process column receives a live slot from every position of that row. `front_init`: the symmetric part of tile (0, 0) of assembled is positive definite.
All inputs are finite; a program needn't handle non-finite values.
Results may differ from the reference program's by a relative error of at most 0.00045.
Values may be sent and summed in bfloat16 or wider, within the bound.
A program may use at most 128 MiB of HBM per device.

```python
import jax
import jax.numpy as jnp
from jax import lax

B = 512
NF = 16384
CT_DEV = 8
GRID_ROWS = 8
GRID_COLS = 16
TILES = 32
TPR = 4
TPC = 2


def shuffled(subkey):
    return jax.random.permutation(subkey, GRID_COLS - 1)


def draw_child_map(key, part):
    key = jax.random.fold_in(key, 1)
    base_key, perm_key, row_key, col_key = jax.random.split(key, 4)
    favored = jax.random.randint(base_key, (GRID_ROWS,), 0, GRID_COLS)
    orders = jax.vmap(shuffled)(jax.random.split(perm_key, GRID_ROWS * GRID_COLS))
    orders = orders.reshape(GRID_ROWS, GRID_COLS, GRID_COLS - 1).astype(jnp.int32)
    leading = jnp.zeros((GRID_ROWS, GRID_COLS, 1), jnp.int32)
    steps_away = jnp.concatenate([leading, orders + 1], axis=2)[:, :, :CT_DEV]
    owners = (favored[:, None, None] + steps_away) % GRID_COLS
    tile_row_block = jax.random.randint(row_key, (GRID_ROWS, GRID_COLS, CT_DEV), 0, TPR)
    tile_col_block = jax.random.randint(col_key, (GRID_ROWS, GRID_COLS, CT_DEV), 0, TPC)
    row_ids = jnp.arange(GRID_ROWS, dtype=jnp.int32)[:, None, None]
    tile_row = tile_row_block * GRID_ROWS + row_ids
    tile_col = tile_col_block * GRID_COLS + owners
    return jnp.stack([tile_row, tile_col], axis=-1).astype(jnp.int32)


def draw_child_counts(key, part):
    key = jax.random.fold_in(key, 2)
    count_key, full_key = jax.random.split(key)
    counts = jax.random.randint(count_key, (GRID_ROWS * GRID_COLS,), max(1, CT_DEV - 3), CT_DEV + 1)
    full_one = jax.random.randint(full_key, (), 0, GRID_ROWS * GRID_COLS)
    counts = jnp.where(jnp.arange(GRID_ROWS * GRID_COLS) == full_one, CT_DEV, counts)
    return counts.reshape(GRID_ROWS, GRID_COLS).astype(jnp.int32)


def draw_child_extent(key, part):
    key = jax.random.fold_in(key, 3)
    levels = jax.random.randint(key, (GRID_ROWS, GRID_COLS, CT_DEV), 2, 9) * (B // 8)
    slot_ids = jnp.arange(CT_DEV, dtype=jnp.int32)[None, None, :]
    return jnp.where(slot_ids == 0, B, levels).astype(jnp.int32)


def draw_front_init(key, part):
    key = jax.random.fold_in(key, 4)
    first_key, second_key, third_key = jax.random.split(key, 3)
    full_shape = (TPR, GRID_ROWS, TPC, GRID_COLS, B, B)
    spread = jnp.clip(0.1 * jax.random.normal(first_key, full_shape, jnp.float32), -0.4, 0.4)
    diagonal_values = jax.random.uniform(second_key, full_shape, jnp.float32, 16.0, 24.0)
    coupling = jax.random.uniform(third_key, (B,), jnp.float32, -0.6, 0.6)
    tile_row = lax.broadcasted_iota(jnp.int32, full_shape, 0) * GRID_ROWS + lax.broadcasted_iota(jnp.int32, full_shape, 1)
    tile_col = lax.broadcasted_iota(jnp.int32, full_shape, 2) * GRID_COLS + lax.broadcasted_iota(jnp.int32, full_shape, 3)
    on_diagonal = (tile_row == tile_col) & (lax.broadcasted_iota(jnp.int32, full_shape, 4) == lax.broadcasted_iota(jnp.int32, full_shape, 5))
    pivot_tile = (tile_row == 0) & (tile_col == 0)
    outer_term = coupling[None, None, None, None, :, None] * coupling[None, None, None, None, None, :]
    return spread + jnp.where(on_diagonal, diagonal_values, 0.0) + jnp.where(pivot_tile, outer_term, 0.0)


def steps_of(own_key, extent, pieces, low, largest):
    gain = 1.0
    for dim, blocks in pieces:
        draws = jax.random.uniform(jax.random.fold_in(jax.random.fold_in(own_key, 6), dim), (blocks,), jnp.float32, low / len(pieces), largest / len(pieces))
        gain = gain * jnp.repeat(jnp.exp(draws), extent[dim] // blocks).reshape((-1,) + (1,) * (len(extent) - 1 - dim))
    return gain


def normal_values(rng, extent, deviation, most, shards=(), kind=jnp.bfloat16):
    array = jax.random.normal(rng, extent, jnp.float32) * deviation
    if len(shards) > 0:
        array = steps_of(rng, extent, shards, -0.22, 0.18) * array
    return jnp.clip(array, min=-most, max=most).astype(kind)


def setup_inputs(seed: int = 0) -> dict:
    splits = jax.random.split(jax.random.key(seed), 6)
    return {
        "front_init": draw_front_init(jax.random.fold_in(splits[5], 71), 0),
        "child_tiles": normal_values(splits[1], (GRID_ROWS, GRID_COLS, CT_DEV, B, B), 0.05, 0.29882812, ((0, 8), (1, 16))),
        "child_map": draw_child_map(jax.random.fold_in(splits[5], 71), 0),
        "child_counts": draw_child_counts(jax.random.fold_in(splits[5], 71), 0),
        "child_extent": draw_child_extent(jax.random.fold_in(splits[5], 71), 0),
    }


def reference(front_init, child_tiles, child_map, child_counts, child_extent):
    front_tiles = front_init.reshape(TILES * TILES, B, B)
    flat_tiles = child_tiles.reshape(-1, B, B)
    flat_map = child_map.reshape(-1, 2)
    slot_ids = jnp.arange(CT_DEV, dtype=jnp.int32)
    alive = (slot_ids[None, None, :] < child_counts[:, :, None]).reshape(-1)
    limits = child_extent.reshape(-1)
    offsets = jnp.arange(B, dtype=jnp.int32)

    def add_child(position, running):
        extent_here = limits[position]
        inside = (offsets[:, None] < extent_here) & (offsets[None, :] < extent_here) & alive[position]
        contribution = jnp.where(inside, flat_tiles[position].astype(jnp.float32), jnp.float32(0.0))
        target_tile = (flat_map[position, 0] * TILES + flat_map[position, 1]).astype(jnp.int32)
        current_tile = lax.dynamic_index_in_dim(running, target_tile, 0, False)
        return lax.dynamic_update_index_in_dim(running, current_tile + contribution, target_tile, 0)
    summed = lax.fori_loop(0, flat_tiles.shape[0], add_child, front_tiles)
    assembled = summed.reshape(TILES, TILES, B, B)
    factor = jnp.linalg.cholesky(assembled[0, 0])
    column_rows = assembled[:, 0].reshape(NF, B)
    solved = jax.scipy.linalg.solve_triangular(factor, column_rows.T, lower=True).T.reshape(TILES, B, B)
    panel_tiles = jnp.concatenate([factor[None], solved[1:]], axis=0)
    flat_panel = panel_tiles.reshape(NF, B)
    dense_front = assembled.transpose(0, 2, 1, 3).reshape(NF, NF)
    update = jnp.dot(flat_panel.astype(jnp.float32), flat_panel.T.astype(jnp.float32), precision=lax.Precision.HIGHEST, preferred_element_type=jnp.float32)
    indices = jnp.arange(NF, dtype=jnp.int32)
    keep_entry = (indices[:, None] >= B) & (indices[None, :] >= B)
    result = jnp.where(keep_entry, dense_front - update, jnp.float32(0.0))
    result = result.reshape(TILES, B, TILES, B).transpose(0, 2, 1, 3).reshape(TPR, GRID_ROWS, TPC, GRID_COLS, B, B)
    return (result, panel_tiles.reshape(TPR, GRID_ROWS, B, B))
```

```python
import functools

import jax
import jax.numpy as jnp
from jax import lax
from jax.experimental import pallas as pl
from jax.experimental.pallas import tpu as pltpu
from jax.sharding import PartitionSpec as P

MESH = pl.DeviceIdType.MESH
HIGH = lax.Precision.HIGHEST
F32 = jnp.float32
BF16 = jnp.bfloat16
B = 512
NB = 128
SLICE = 32
COLS = 16
ROWS = 8


def dot_nt(a, b, precision=HIGH):
    return lax.dot_general(
        a, b, (((1,), (1,)), ((), ())), precision=precision, preferred_element_type=F32
    )


def dot_nn(a, b, precision=HIGH):
    return lax.dot_general(
        a, b, (((1,), (0,)), ((), ())), precision=precision, preferred_element_type=F32
    )


def wide(x):
    return jnp.broadcast_to(x, (8, NB))


def factor_block(s):
    lane = lax.broadcasted_iota(jnp.int32, (8, NB), 1)
    sub = lax.broadcasted_iota(jnp.int32, (8, NB), 0)
    groups = NB // 8
    rows = [s[8 * p : 8 * p + 8, :] for p in range(groups)]
    eye = [jnp.where(lane == sub + 8 * p, 1.0, 0.0).astype(F32) for p in range(groups)]
    out_u, out_v = [], []
    for p in range(groups):
        r, e = rows[p], eye[p]
        cols = [wide(r[:, 8 * p + t : 8 * p + t + 1]) for t in range(8)]
        inv = [jnp.where(sub == t, 1.0, 0.0).astype(F32) for t in range(8)]
        pivots = None
        for t in range(8):
            pivot = wide(cols[t][t : t + 1, :])
            pivots = pivot if t == 0 else jnp.where(sub == t, pivot, pivots)
            m = jnp.where(sub > t, cols[t], 0.0) * (1.0 / pivot)
            for j in range(t + 1, 8):
                cols[j] = cols[j] - m * wide(cols[j][t : t + 1, :])
            for j in range(t + 1):
                inv[j] = inv[j] - m * wide(inv[j][t : t + 1, :])
        scale = lax.rsqrt(pivots)
        u = jnp.zeros_like(r)
        v = jnp.zeros_like(e)
        for t in range(8):
            u = u + inv[t] * wide(r[t : t + 1, :])
            v = v + inv[t] * wide(e[t : t + 1, :])
        u = u * scale
        v = v * scale
        out_u.append(jnp.where(lane >= sub + 8 * p, u, 0.0))
        out_v.append(v)
        if p < groups - 1:
            ut = jnp.transpose(u)
            for q in range(p + 1, groups):
                coef = ut[8 * q : 8 * q + 8, :]
                for t in range(8):
                    c = wide(coef[:, t : t + 1])
                    rows[q] = rows[q] - c * wide(u[t : t + 1, :])
                    eye[q] = eye[q] - c * wide(v[t : t + 1, :])
    return jnp.concatenate(out_u, 0), jnp.concatenate(out_v, 0)


def factor_step(j, s, l_ref, v_ref):
    a, b = NB * j, NB * j + NB
    u, v = factor_block(s[a:b, a:b])
    l_ref[a:b, a:b] = jnp.transpose(u)
    v_ref[a:b, a:b] = v
    if j:
        w = dot_nn(l_ref[a:b, 0:a], v_ref[0:a, 0:a])
        v_ref[a:b, 0:a] = -dot_nn(v, w)
    if b < B:
        low = dot_nt(s[b:B, a:b], v)
        l_ref[b:B, a:b] = low
        s[b:B, b:B] = s[b:B, b:B] - dot_nt(low, low)


def main_kernel(
    tab,
    kids_hbm,
    front_hbm,
    land,
    panel_hbm,
    need_hbm,
    kids,
    bucket,
    land0,
    fslice,
    pivot,
    col0,
    s,
    l_ref,
    v_ref,
    panel,
    own_need,
    loc,
    cut_s,
    cut_r,
    fs_s,
    fs_r,
    pr_s,
    pr_r,
    pg_s,
    pg_r,
    px,
    ag_s,
    ag_r,
    ax,
    bk_s,
    bk_r,
    nd_s,
    nd_r,
):
    row = lax.axis_index("row")
    col = lax.axis_index("col")
    zy = col // 2
    core = col % 2

    def remote(src, dst, ss, rs, to):
        return pltpu.make_async_remote_copy(
            src_ref=src, dst_ref=dst, send_sem=ss, recv_sem=rs, device_id=to, device_id_type=MESH
        )

    def mate(d):
        return lax.rem(col + d, COLS)

    def kin(d):
        return lax.rem(zy + d, ROWS)

    def fellow(d):
        return lax.rem(row + d, ROWS)

    sibling = (row, zy * 2 + 1 - core)

    load = pltpu.make_async_copy(kids_hbm, kids, loc.at[0])
    load.start()

    barrier = pltpu.get_barrier_semaphore()

    @pl.loop(1, COLS)
    def _(d):
        pl.semaphore_signal(barrier, inc=1, device_id=(row, mate(d)), device_id_type=MESH)

    @pl.loop(1, ROWS)
    def _(d):
        pl.semaphore_signal(barrier, inc=1, device_id=(fellow(d), col), device_id_type=MESH)

    pl.semaphore_wait(barrier, COLS - 1 + ROWS - 1)

    def front_part(k):
        return front_hbm.at[:, 0, pl.ds(pl.multiple_of(k * SLICE, SLICE), SLICE), :]

    def front_cut(d):
        return remote(front_part(mate(d)), fslice, fs_s.at[d], fs_r, (row, mate(d)))

    front_own = pltpu.make_async_copy(front_part(col), fslice, loc.at[1])

    @pl.when(col == 0)
    def _():
        front_own.start()

        @pl.loop(1, COLS)
        def _(d):
            front_cut(d).start()

    load.wait()

    def pack(k):
        slot = (tab[col, k] >> 16) & 7

        @pl.loop(0, 4)
        def _(q):
            part = pl.ds(pl.multiple_of(q * NB, NB), NB)
            bucket[k, part, :] = kids[slot, part, :]

    pack(0)

    def cut(d):
        k = mate(d)
        return remote(
            bucket.at[0, pl.ds(pl.multiple_of(k * SLICE, SLICE), SLICE), :],
            land0.at[col],
            cut_s.at[d],
            cut_r.at[col],
            (row, k),
        )

    def cut_from(d):
        k = mate(d)
        return remote(bucket.at[0, 0:SLICE, :], land0.at[k], cut_s.at[d], cut_r.at[k], (row, k))

    @pl.loop(1, COLS)
    def _(d):
        cut(d).start()

    land0[col] = bucket[0, pl.ds(pl.multiple_of(col * SLICE, SLICE), SLICE), :]

    @pl.loop(1, COLS)
    def _(k):
        pack(k)

    @pl.loop(1, COLS)
    def _(d):
        cut_from(d).wait_recv()

    @pl.when(col == 0)
    def _():
        front_own.wait()

    @pl.when(col != 0)
    def _():
        front_cut(1).wait_recv()

    at_row = col * SLICE + lax.broadcasted_iota(jnp.int32, (SLICE, B), 0)
    at_col = lax.broadcasted_iota(jnp.int32, (SLICE, B), 1)

    @pl.loop(0, COLS)
    def _(k):
        code = tab[k, 0]
        extent = code & 1023
        tile = (code >> 12) & 7
        inside = (at_row < extent) & (at_col < extent)
        part = jnp.where(inside, land0[k].astype(F32), 0.0)
        for a in range(4):
            fslice[a] = fslice[a] + jnp.where(tile == 2 * a, part, 0.0)

    def pivot_row(d):
        here = pivot.at[zy, core]
        return remote(here, here, pr_s.at[d], pr_r, (fellow(d), col))

    @pl.when(row == 0)
    def _():
        pivot[zy, core] = fslice[0]

        @pl.loop(1, ROWS)
        def _(d):
            pivot_row(d).start()

    @pl.when(row != 0)
    def _():
        pivot_row(1).wait_recv()

    def pivot_col(d, there):
        here = pivot.at[there, core]
        return remote(here, here, pg_s.at[d], pg_r.at[there], (row, kin(d) * 2 + core))

    @pl.loop(1, ROWS)
    def _(d):
        pivot_col(d, zy).start()

    for a in range(4):
        col0[a, zy, core] = fslice[a]

    def gather(d, there):
        here = col0.at[:, there, core]
        return remote(here, here, ag_s.at[d], ag_r.at[there], (row, kin(d) * 2 + core))

    @pl.loop(1, ROWS)
    def _(d):
        gather(d, zy).start()

    @pl.loop(1, ROWS)
    def _(d):
        pivot_col(d, kin(d)).wait_recv()

    def pivot_swap(which):
        here = pivot.at[:, which]
        return remote(here, here, px.at[0], px.at[1], sibling)

    pivot_swap(core).start()

    def bulk(d):
        k = mate(d)
        return remote(bucket.at[k], land.at[col], bk_s.at[d], bk_r.at[col], (row, k))

    def bulk_from(d):
        k = mate(d)
        return remote(bucket.at[k], land.at[k], bk_s.at[d], bk_r.at[k], (row, k))

    @pl.loop(1, COLS)
    def _(d):
        bulk(d).start()

    keep_own = pltpu.make_async_copy(bucket.at[col], land.at[col], loc.at[2])
    keep_own.start()

    pivot_swap(1 - core).wait_recv()
    for i in range(4):
        for j in range(4):
            f = pivot[2 * i : 2 * i + 2, :, :, NB * j : NB * j + NB].reshape(NB, NB)
            g = pivot[2 * j : 2 * j + 2, :, :, NB * i : NB * i + NB].reshape(NB, NB)
            s[NB * i : NB * i + NB, NB * j : NB * j + NB] = 0.5 * (f + jnp.transpose(g))
    l_ref[...] = jnp.zeros_like(l_ref)
    v_ref[...] = jnp.zeros_like(v_ref)

    def gather_swap(which):
        here = col0.at[:, :, which]
        return remote(here, here, ax.at[0], ax.at[1], sibling)

    for j in range(4):
        factor_step(j, s, l_ref, v_ref)
        if j == 2:

            @pl.loop(1, ROWS)
            def _(d):
                gather(d, kin(d)).wait_recv()

            gather_swap(core).start()

    gather_swap(1 - core).wait_recv()

    @pl.loop(0, 16)
    def _(i):
        a = i // 4
        q = i % 4
        part = col0[a, pl.ds(q * 2, 2)].reshape(NB, B)
        out = pl.ds(pl.multiple_of(q * NB, NB), NB)
        panel[a, out, :] = dot_nt(part, v_ref[...])

    @pl.when(row == 0)
    def _():
        panel[0] = l_ref[...]

    panel_out = pltpu.make_async_copy(panel, panel_hbm, loc.at[3])
    panel_out.start()

    def need(d):
        return remote(own_need, need_hbm, nd_s.at[d], nd_r, (fellow(d), col))

    need_own = pltpu.make_async_copy(own_need, need_hbm, loc.at[4])

    @pl.when(row == col % ROWS)
    def _():
        for b in range(2):

            @pl.loop(0, 4)
            def _(q):
                part = pl.ds(pl.multiple_of(q * NB, NB), NB)
                own_need[b, part, :] = panel[col // ROWS + 2 * b, part, :].astype(BF16)

        need_own.start()

        @pl.loop(1, ROWS)
        def _(d):
            need(d).start()

        need_own.wait()

        @pl.loop(1, ROWS)
        def _(d):
            need(d).wait_send()

    @pl.when(row != col % ROWS)
    def _():
        need(1).wait_recv()

    @pl.when(row == 0)
    def _():
        @pl.loop(1, ROWS)
        def _(d):
            pivot_row(d).wait_send()

    @pl.when(col == 0)
    def _():
        @pl.loop(1, COLS)
        def _(d):
            front_cut(d).wait_send()

    pivot_swap(core).wait_send()
    gather_swap(core).wait_send()

    @pl.loop(1, ROWS)
    def _(d):
        pivot_col(d, zy).wait_send()
        gather(d, zy).wait_send()

    @pl.loop(1, COLS)
    def _(d):
        cut(d).wait_send()
        bulk(d).wait_send()

    @pl.loop(1, COLS)
    def _(d):
        bulk_from(d).wait_recv()

    keep_own.wait()
    panel_out.wait()


def main_call(tab, kids, front):
    any_space = pl.BlockSpec(memory_space=pl.ANY)
    dma = pltpu.SemaphoreType.DMA
    return pl.pallas_call(
        main_kernel,
        out_shape=(
            jax.ShapeDtypeStruct((COLS, B, B), BF16),
            jax.ShapeDtypeStruct((4, B, B), F32),
            jax.ShapeDtypeStruct((2, B, B), BF16),
        ),
        in_specs=[pl.BlockSpec(memory_space=pltpu.SMEM), any_space, any_space],
        out_specs=(any_space,) * 3,
        scratch_shapes=[
            pltpu.VMEM((8, B, B), BF16),
            pltpu.VMEM((COLS, B, B), BF16),
            pltpu.VMEM((COLS, SLICE, B), BF16),
            pltpu.VMEM((4, SLICE, B), F32),
            pltpu.VMEM((8, 2, SLICE, B), F32),
            pltpu.VMEM((4, 8, 2, SLICE, B), F32),
            pltpu.VMEM((B, B), F32),
            pltpu.VMEM((B, B), F32),
            pltpu.VMEM((B, B), F32),
            pltpu.VMEM((4, B, B), F32),
            pltpu.VMEM((2, B, B), BF16),
            dma((5,)),
            dma((COLS,)),
            dma((COLS,)),
            dma((COLS,)),
            dma,
            dma((ROWS,)),
            dma,
            dma((ROWS,)),
            dma((ROWS,)),
            dma((2,)),
            dma((ROWS,)),
            dma((ROWS,)),
            dma((2,)),
            dma((COLS,)),
            dma((COLS,)),
            dma((ROWS,)),
            dma,
        ],
        compiler_params=pltpu.CompilerParams(
            collective_id=0, has_side_effects=True, vmem_limit_bytes=56 * 2**20
        ),
        cost_estimate=pl.CostEstimate(
            flops=2 * 5 * B**3, bytes_accessed=24 * 2**20, transcendentals=0
        ),
    )(tab, kids, front)


def final_kernel(tab, front, panel, need, land, schur, panel_out, kids, sem):
    row = lax.axis_index("row")
    col = lax.axis_index("col")
    t = pl.program_id(0)
    a = t // 2
    b = t % 2

    def fetch(k):
        return pltpu.make_async_copy(land.at[k], kids.at[k], sem.at[k])

    @pl.when(t == 0)
    def _():
        @pl.loop(0, COLS)
        def _(k):
            @pl.when(tab[k, col] != 0)
            def _():
                fetch(k).start()

    @pl.when(b == 0)
    def _():
        panel_out[...] = panel[...]

    i = a * ROWS + row
    j = b * COLS + col
    keep = (i > 0) & (j > 0)

    @pl.loop(0, 4)
    def _(q):
        part = pl.ds(pl.multiple_of(q * NB, NB), NB)
        p = panel[0, part, :]
        hi = p.astype(BF16)
        lo = (p - hi.astype(F32)).astype(BF16)
        update = dot_nt(hi, need[0], None) + dot_nt(lo, need[0], None)
        schur[0, part, :] = jnp.where(keep, front[0, part, :] - update, 0.0)

    at_row = lax.broadcasted_iota(jnp.int32, (NB, B), 0)
    at_col = lax.broadcasted_iota(jnp.int32, (NB, B), 1)

    @pl.loop(0, COLS)
    def _(k):
        code = tab[k, col]
        extent = code & 1023

        @pl.when((code != 0) & (((code >> 12) & 7) == t))
        def _():
            fetch(k).wait()

            @pl.loop(0, 4)
            def _(q):
                part = pl.ds(pl.multiple_of(q * NB, NB), NB)
                inside = (at_row + q * NB < extent) & (at_col < extent) & keep
                schur[0, part, :] = schur[0, part, :] + jnp.where(
                    inside, kids[k, part, :].astype(F32), 0.0
                )


def final_call(tab, front, panel, need, land):
    return pl.pallas_call(
        final_kernel,
        out_shape=(
            jax.ShapeDtypeStruct((8, B, B), F32),
            jax.ShapeDtypeStruct((4, B, B), F32),
        ),
        grid_spec=pltpu.PrefetchScalarGridSpec(
            num_scalar_prefetch=1,
            grid=(8,),
            in_specs=[
                pl.BlockSpec((1, B, B), lambda t, tab: (t, 0, 0)),
                pl.BlockSpec((1, B, B), lambda t, tab: (t // 2, 0, 0)),
                pl.BlockSpec((1, B, B), lambda t, tab: (t % 2, 0, 0)),
                pl.BlockSpec(memory_space=pl.ANY),
            ],
            out_specs=[
                pl.BlockSpec((1, B, B), lambda t, tab: (t, 0, 0)),
                pl.BlockSpec((1, B, B), lambda t, tab: (t // 2, 0, 0)),
            ],
            scratch_shapes=[pltpu.VMEM((COLS, B, B), BF16), pltpu.SemaphoreType.DMA((COLS,))],
        ),
        compiler_params=pltpu.CompilerParams(vmem_limit_bytes=56 * 2**20),
        cost_estimate=pl.CostEstimate(
            flops=4 * 8 * B**3, bytes_accessed=36 * 2**20, transcendentals=0
        ),
    )(tab, front, panel, need, land)


def per_device(front_init, child_tiles, child_map, child_counts, child_extent):
    row = lax.axis_index("row")
    maps = lax.dynamic_index_in_dim(child_map, row, 0, False)
    counts = lax.dynamic_index_in_dim(child_counts, row, 0, False)
    extents = lax.dynamic_index_in_dim(child_extent, row, 0, False)
    slots = jnp.arange(8, dtype=jnp.int32)[None, :]
    tile = maps[:, :, 0] // ROWS * 2 + maps[:, :, 1] // COLS
    code = (1 << 20) + slots * (1 << 16) + tile * (1 << 12) + extents
    code = jnp.where(slots < counts[:, None], code, 0)
    dests = jnp.arange(COLS, dtype=jnp.int32)[None, None, :]
    hit = (maps[:, :, 1] % COLS)[:, :, None] == dests
    tab = jnp.sum(jnp.where(hit, code[:, :, None], 0), axis=1)
    kids = child_tiles.reshape(8, B, B)
    land, panel, need = main_call(tab, kids, front_init.reshape(4, 2, B, B))
    schur, panel = final_call(tab, front_init.reshape(8, B, B), panel, need, land)
    return schur.reshape(4, 1, 2, 1, B, B), panel.reshape(4, 1, B, B)


def solution(mesh):
    in_specs = (
        P(None, "row", None, "col", None, None),
        P("row", "col", None, None, None),
        P(),
        P(),
        P(),
    )
    out_specs = (P(None, "row", None, "col", None, None), P(None, "row", None, None))
    return jax.shard_map(
        per_device, mesh=mesh, in_specs=in_specs, out_specs=out_specs, check_vma=False
    )
```

```python
import functools

import jax
import jax.numpy as jnp
from jax import lax
from jax.experimental import pallas as pl
from jax.experimental.pallas import tpu as pltpu
from jax.sharding import PartitionSpec as P

MESH = pl.DeviceIdType.MESH
HIGH = lax.Precision.HIGHEST
F32 = jnp.float32
BF16 = jnp.bfloat16
B = 512
NB = 128
SLICE = 32
COLS = 16
ROWS = 8
HOOKS = (0, 1)
BULK = ((), (), (), (1, 2, 3), (4, 5, 12, 13, 8, 9), (6, 7, 14, 15, 10, 11))


def dot_nt(a, b, precision=HIGH):
    return lax.dot_general(
        a, b, (((1,), (1,)), ((), ())), precision=precision, preferred_element_type=F32
    )


def dot_nn(a, b, precision=HIGH):
    return lax.dot_general(
        a, b, (((1,), (0,)), ((), ())), precision=precision, preferred_element_type=F32
    )


def wide(x):
    return jnp.broadcast_to(x, (8, NB))


def factor_block(s):
    lane = lax.broadcasted_iota(jnp.int32, (8, NB), 1)
    sub = lax.broadcasted_iota(jnp.int32, (8, NB), 0)
    groups = NB // 8
    rows = [s[8 * p : 8 * p + 8, :] for p in range(groups)]
    eye = [jnp.where(lane == sub + 8 * p, 1.0, 0.0).astype(F32) for p in range(groups)]
    out_u, out_v = [], []
    for p in range(groups):
        r, e = rows[p], eye[p]
        cols = [wide(r[:, 8 * p + t : 8 * p + t + 1]) for t in range(8)]
        inv = [jnp.where(sub == t, 1.0, 0.0).astype(F32) for t in range(8)]
        pivots = None
        for t in range(8):
            pivot = wide(cols[t][t : t + 1, :])
            pivots = pivot if t == 0 else jnp.where(sub == t, pivot, pivots)
            m = jnp.where(sub > t, cols[t], 0.0) * (1.0 / pivot)
            for j in range(t + 1, 8):
                cols[j] = cols[j] - m * wide(cols[j][t : t + 1, :])
            for j in range(t + 1):
                inv[j] = inv[j] - m * wide(inv[j][t : t + 1, :])
        scale = lax.rsqrt(pivots)
        u = jnp.zeros_like(r)
        v = jnp.zeros_like(e)
        for t in range(8):
            u = u + inv[t] * wide(r[t : t + 1, :])
            v = v + inv[t] * wide(e[t : t + 1, :])
        u = u * scale
        v = v * scale
        out_u.append(jnp.where(lane >= sub + 8 * p, u, 0.0))
        out_v.append(v)
        if p < groups - 1:
            ut = jnp.transpose(u)
            for q in range(p + 1, groups):
                coef = ut[8 * q : 8 * q + 8, :]
                for t in range(8):
                    c = wide(coef[:, t : t + 1])
                    rows[q] = rows[q] - c * wide(u[t : t + 1, :])
                    eye[q] = eye[q] - c * wide(v[t : t + 1, :])
    return jnp.concatenate(out_u, 0), jnp.concatenate(out_v, 0)


def factor_step(j, s, l_ref, v_ref):
    a, b = NB * j, NB * j + NB
    u, v = factor_block(s[a:b, a:b])
    l_ref[a:b, a:b] = jnp.transpose(u)
    v_ref[a:b, a:b] = v
    if j:
        w = dot_nn(l_ref[a:b, 0:a], v_ref[0:a, 0:a])
        v_ref[a:b, 0:a] = -dot_nn(v, w)
    if b < B:
        low = dot_nt(s[b:B, a:b], v)
        l_ref[b:B, a:b] = low
        s[b:B, b:B] = s[b:B, b:B] - dot_nt(low, low)


def main_kernel(
    tab,
    kids_hbm,
    front_hbm,
    land,
    panel_hbm,
    part_hbm,
    kids,
    bucket,
    land0,
    fslice,
    pivot,
    col0,
    s,
    l_ref,
    v_ref,
    panel,
    own_need,
    need,
    front,
    w_hi,
    w_lo,
    loc,
    f_in,
    f_out,
    cut_s,
    cut_r,
    fs_s,
    fs_r,
    ft_s,
    ft_r,
    pr_s,
    pr_r,
    pg_s,
    pg_r,
    px,
    ag_s,
    ag_r,
    ay,
    ax,
    bk_s,
    bk_r,
    nd_s,
    nd_t,
    nd_r,
):
    row = lax.axis_index("row")
    col = lax.axis_index("col")
    zy = col // 2
    core = col % 2
    z = zy // 2
    yh = zy % 2
    x = row % 4
    yl = row // 4

    def remote(src, dst, ss, rs, to):
        return pltpu.make_async_remote_copy(
            src_ref=src, dst_ref=dst, send_sem=ss, recv_sem=rs, device_id=to, device_id_type=MESH
        )

    def kin(d):
        z = lax.rem(zy // 2 + d // 2, 4)
        return z * 2 + lax.rem(zy + d, 2)

    def mate(d):
        return kin(d // 2) * 2 + lax.rem(core + d, 2)

    def fellow(d):
        x = lax.rem(row + d, 4)
        return lax.rem(row // 4 + d // 4, 2) * 4 + x

    sibling = (row, zy * 2 + 1 - core)

    load = pltpu.make_async_copy(kids_hbm, kids, loc.at[0])
    load.start()

    barrier = pltpu.get_barrier_semaphore()

    @pl.loop(1, COLS)
    def _(d):
        pl.semaphore_signal(barrier, inc=1, device_id=(row, mate(d)), device_id_type=MESH)

    @pl.loop(1, ROWS)
    def _(d):
        pl.semaphore_signal(barrier, inc=1, device_id=(fellow(d), col), device_id_type=MESH)

    pl.semaphore_wait(barrier, COLS - 1 + ROWS - 1)

    def first_part(k):
        return front_hbm.at[0, 0, pl.ds(pl.multiple_of(k * SLICE, SLICE), SLICE), :]

    def rest_part(k):
        return front_hbm.at[1:4, 0, pl.ds(pl.multiple_of(k * SLICE, SLICE), SLICE), :]

    def first_cut(d):
        k = mate(d)
        return remote(first_part(k), fslice.at[0], fs_s.at[d], fs_r, (row, k))

    def rest_cut(d):
        k = mate(d)
        return remote(rest_part(k), fslice.at[1:4], ft_s.at[d], ft_r, (row, k))

    first_own = pltpu.make_async_copy(first_part(col), fslice.at[0], loc.at[1])
    rest_own = pltpu.make_async_copy(rest_part(col), fslice.at[1:4], loc.at[4])

    @pl.when(col == 0)
    def _():
        first_own.start()

        @pl.loop(1, COLS)
        def _(d):
            first_cut(d).start()

    load.wait()

    def pack(k):
        slot = (tab[col, k] >> 16) & 7

        @pl.loop(0, 4)
        def _(q):
            part = pl.ds(pl.multiple_of(q * NB, NB), NB)
            bucket[k, part, :] = kids[slot, part, :]

    pack(0)

    def cut(d):
        k = mate(d)
        return remote(
            bucket.at[0, pl.ds(pl.multiple_of(k * SLICE, SLICE), SLICE), :],
            land0.at[col],
            cut_s.at[d],
            cut_r.at[col],
            (row, k),
        )

    def cut_from(d):
        k = mate(d)
        return remote(bucket.at[0, 0:SLICE, :], land0.at[k], cut_s.at[d], cut_r.at[k], (row, k))

    @pl.loop(1, COLS)
    def _(d):
        cut(d).start()

    def bulk(d):
        k = mate(d)
        return remote(bucket.at[k], land.at[col], bk_s.at[d], bk_r.at[col], (row, k))

    def bulk_from(d):
        k = mate(d)
        return remote(bucket.at[k], land.at[k], bk_s.at[d], bk_r.at[k], (row, k))

    keep_own = pltpu.make_async_copy(bucket.at[col], land.at[col], loc.at[2])

    def start_bulk(stage):
        for d in BULK[stage]:
            bulk(d).start()

    land0[col] = bucket[0, pl.ds(pl.multiple_of(col * SLICE, SLICE), SLICE), :]

    @pl.loop(1, COLS)
    def _(k):
        pack(k)

    keep_own.start()

    @pl.when(col == 0)
    def _():
        rest_own.start()

        @pl.loop(1, COLS)
        def _(d):
            rest_cut(d).start()

    def fetch(t):
        return pltpu.make_async_copy(front_hbm.at[t // 2, t % 2], front.at[t], f_in.at[t])

    for t in range(8):
        fetch(t).start()

    start_bulk(0)

    @pl.loop(1, COLS)
    def _(d):
        cut_from(d).wait_recv()

    @pl.when(col == 0)
    def _():
        first_own.wait()

    @pl.when(col != 0)
    def _():
        first_cut(1).wait_recv()

    at_row = col * SLICE + lax.broadcasted_iota(jnp.int32, (SLICE, B), 0)
    at_col = lax.broadcasted_iota(jnp.int32, (SLICE, B), 1)

    def add_kids(tiles):
        @pl.loop(0, COLS)
        def _(k):
            code = tab[k, 0]
            extent = code & 1023
            tile = (code >> 12) & 7
            inside = (at_row < extent) & (at_col < extent)
            part = jnp.where(inside, land0[k].astype(F32), 0.0)
            for a in tiles:
                fslice[a] = fslice[a] + jnp.where(tile == 2 * a, part, 0.0)

    add_kids((0,))

    def pivot_row(d):
        here = pivot.at[zy, core]
        return remote(here, here, pr_s.at[d], pr_r, (fellow(d), col))

    @pl.when(row == 0)
    def _():
        pivot[zy, core] = fslice[0]

        @pl.loop(1, ROWS)
        def _(d):
            pivot_row(d).start()

    @pl.when(row != 0)
    def _():
        pivot_row(1).wait_recv()

    def pivot_col(d, there):
        here = pivot.at[there, core]
        return remote(here, here, pg_s.at[d], pg_r.at[there], (row, kin(d) * 2 + core))

    @pl.loop(1, ROWS)
    def _(d):
        pivot_col(d, zy).start()

    start_bulk(1)

    @pl.when(col == 0)
    def _():
        rest_own.wait()

    @pl.when(col != 0)
    def _():
        rest_cut(1).wait_recv()

    add_kids((1, 2, 3))

    for a in range(4):
        col0[a, z, yh, core] = fslice[a]

    def gather(d, there):
        here = col0.at[:, there, yh, core]
        to = (row, lax.rem(z + d, 4) * 4 + yh * 2 + core)
        return remote(here, here, ag_s.at[d], ag_r.at[there], to)

    @pl.loop(1, 4)
    def _(d):
        gather(d, z).start()

    start_bulk(2)

    @pl.loop(1, ROWS)
    def _(d):
        pivot_col(d, kin(d)).wait_recv()

    def pivot_swap(which):
        here = pivot.at[:, which]
        return remote(here, here, px.at[0], px.at[1], sibling)

    pivot_swap(core).start()

    start_bulk(3)

    pivot_swap(1 - core).wait_recv()
    for i in range(4):
        for j in range(4):
            f = pivot[2 * i : 2 * i + 2, :, :, NB * j : NB * j + NB].reshape(NB, NB)
            g = pivot[2 * j : 2 * j + 2, :, :, NB * i : NB * i + NB].reshape(NB, NB)
            s[NB * i : NB * i + NB, NB * j : NB * j + NB] = 0.5 * (f + jnp.transpose(g))
    l_ref[...] = jnp.zeros_like(l_ref)
    v_ref[...] = jnp.zeros_like(v_ref)

    def cross(side):
        here = col0.at[:, :, side, core]
        return remote(here, here, ay.at[0], ay.at[1], (row, z * 4 + (1 - yh) * 2 + core))

    def gather_swap(side, which, n):
        here = col0.at[:, :, side, which]
        return remote(here, here, ax.at[2 * n], ax.at[2 * n + 1], sibling)

    def relay_cross():
        @pl.loop(1, 4)
        def _(d):
            gather(d, lax.rem(z + d, 4)).wait_recv()

        cross(yh).start()
        gather_swap(yh, core, 0).start()
        start_bulk(4)

    def relay_swap():
        cross(1 - yh).wait_recv()
        gather_swap(1 - yh, core, 1).start()
        start_bulk(5)

    hooks = {HOOKS[0]: relay_cross, HOOKS[1]: relay_swap}
    for j in range(4):
        factor_step(j, s, l_ref, v_ref)
        if j in hooks:
            hooks[j]()

    gather_swap(yh, 1 - core, 0).wait_recv()
    gather_swap(1 - yh, 1 - core, 1).wait_recv()

    for i in range(4):
        for j in range(i, 4):
            here = (slice(NB * i, NB * i + NB), slice(NB * j, NB * j + NB))
            w = jnp.transpose(v_ref[here[1], here[0]])
            hi = w.astype(BF16)
            w_hi[here] = hi
            w_lo[here] = (w - hi.astype(F32)).astype(BF16)
    for w in (w_hi, w_lo):
        w[NB : 2 * NB, 0:NB] = jnp.zeros((NB, NB), BF16)
        w[3 * NB : B, 2 * NB : 3 * NB] = jnp.zeros((NB, NB), BF16)

    half = B // 2

    @pl.loop(0, 4)
    def _(a):
        part = col0[a].reshape(B, B)
        hi = part.astype(BF16)
        lo = (part - hi.astype(F32)).astype(BF16)
        for c0, depth in ((0, half), (half, B)):
            wh = w_hi[0:depth, c0 : c0 + half]
            wl = w_lo[0:depth, c0 : c0 + half]
            panel[a, :, c0 : c0 + half] = (
                dot_nn(hi[:, 0:depth], wh, None)
                + dot_nn(hi[:, 0:depth], wl, None)
                + dot_nn(lo[:, 0:depth], wh, None)
            )

    @pl.when(row == 0)
    def _():
        panel[0] = l_ref[...]

    panel_out = pltpu.make_async_copy(panel, panel_hbm, loc.at[3])
    panel_out.start()

    root = col % ROWS

    def piece(ref, g):
        return ref.at[:, pl.ds(pl.multiple_of(g * NB, NB), NB), :]

    def beside(d):
        return lax.rem(x + d, 4)

    def deal(d):
        g = beside(d)
        to = (yl * 4 + g, col)
        return remote(piece(own_need, g), piece(need, g), nd_t.at[d], nd_r.at[g], to)

    def hand(d, ref, g):
        to = (yl * 4 + beside(d), col)
        return remote(piece(ref, g), piece(need, g), nd_s.at[d], nd_r.at[g], to)

    def over(ref):
        to = ((1 - yl) * 4 + x, col)
        return remote(piece(ref, x), piece(need, x), nd_s.at[0], nd_r.at[x], to)

    need_own = pltpu.make_async_copy(own_need, need, loc.at[5])

    @pl.when(row == root)
    def _():
        for b in range(2):
            for q in range(4):
                part = panel[col // ROWS + 2 * b, NB * q : NB * q + NB, :]
                own_need[b, :, NB * q : NB * q + NB] = jnp.transpose(part).astype(BF16)

        over(own_need).start()

        @pl.loop(1, 4)
        def _(d):
            deal(d).start()

        @pl.loop(1, 4)
        def _(d):
            hand(d, own_need, x).start()

        need_own.start()
        need_own.wait()
        over(own_need).wait_send()

        @pl.loop(1, 4)
        def _(d):
            deal(d).wait_send()
            hand(d, own_need, x).wait_send()

    @pl.when((row != root) & (yl == root // 4))
    def _():
        hand(1, need, x).wait_recv()
        over(need).start()

        @pl.loop(1, 4)
        def _(d):
            @pl.when(beside(d) != root % 4)
            def _():
                hand(d, need, x).start()

        @pl.loop(1, 4)
        def _(d):
            hand(d, need, beside(d)).wait_recv()

        over(need).wait_send()

        @pl.loop(1, 4)
        def _(d):
            @pl.when(beside(d) != root % 4)
            def _():
                hand(d, need, x).wait_send()

    @pl.when(yl != root // 4)
    def _():
        hand(1, need, x).wait_recv()

        @pl.loop(1, 4)
        def _(d):
            hand(d, need, x).start()

        @pl.loop(1, 4)
        def _(d):
            hand(d, need, beside(d)).wait_recv()

        @pl.loop(1, 4)
        def _(d):
            hand(d, need, x).wait_send()

    for t in range(8):
        fetch(t).wait()

    def put(t):
        return pltpu.make_async_copy(front.at[t], part_hbm.at[t], f_out.at[t])

    @pl.loop(0, 8)
    def _(t):
        a = t // 2
        b = t % 2
        keep = (a * ROWS + row > 0) & (b * COLS + col > 0)
        p = panel[a]
        hi = p.astype(BF16)
        lo = (p - hi.astype(F32)).astype(BF16)
        update = dot_nn(hi, need[b], None) + dot_nn(lo, need[b], None)
        front[t] = jnp.where(keep, front[t] - update, 0.0)
        put(t).start()

    @pl.when(row == 0)
    def _():
        @pl.loop(1, ROWS)
        def _(d):
            pivot_row(d).wait_send()

    @pl.when(col == 0)
    def _():
        @pl.loop(1, COLS)
        def _(d):
            first_cut(d).wait_send()
            rest_cut(d).wait_send()

    pivot_swap(core).wait_send()
    cross(yh).wait_send()
    gather_swap(yh, core, 0).wait_send()
    gather_swap(1 - yh, core, 1).wait_send()

    @pl.loop(1, ROWS)
    def _(d):
        pivot_col(d, zy).wait_send()

    @pl.loop(1, 4)
    def _(d):
        gather(d, z).wait_send()

    @pl.loop(1, COLS)
    def _(d):
        cut(d).wait_send()
        bulk(d).wait_send()

    @pl.loop(1, COLS)
    def _(d):
        bulk_from(d).wait_recv()

    keep_own.wait()
    panel_out.wait()
    for t in range(8):
        put(t).wait()


def main_call(tab, kids, front):
    any_space = pl.BlockSpec(memory_space=pl.ANY)
    dma = pltpu.SemaphoreType.DMA
    return pl.pallas_call(
        main_kernel,
        out_shape=(
            jax.ShapeDtypeStruct((COLS, B, B), BF16),
            jax.ShapeDtypeStruct((4, B, B), F32),
            jax.ShapeDtypeStruct((8, B, B), F32),
        ),
        in_specs=[pl.BlockSpec(memory_space=pltpu.SMEM), any_space, any_space],
        out_specs=(any_space,) * 3,
        scratch_shapes=[
            pltpu.VMEM((8, B, B), BF16),
            pltpu.VMEM((COLS, B, B), BF16),
            pltpu.VMEM((COLS, SLICE, B), BF16),
            pltpu.VMEM((4, SLICE, B), F32),
            pltpu.VMEM((8, 2, SLICE, B), F32),
            pltpu.VMEM((4, 4, 2, 2, SLICE, B), F32),
            pltpu.VMEM((B, B), F32),
            pltpu.VMEM((B, B), F32),
            pltpu.VMEM((B, B), F32),
            pltpu.VMEM((4, B, B), F32),
            pltpu.VMEM((2, B, B), BF16),
            pltpu.VMEM((2, B, B), BF16),
            pltpu.VMEM((8, B, B), F32),
            pltpu.VMEM((B, B), BF16),
            pltpu.VMEM((B, B), BF16),
            dma((6,)),
            dma((8,)),
            dma((8,)),
            dma((COLS,)),
            dma((COLS,)),
            dma((COLS,)),
            dma,
            dma((COLS,)),
            dma,
            dma((ROWS,)),
            dma,
            dma((ROWS,)),
            dma((ROWS,)),
            dma((2,)),
            dma((4,)),
            dma((4,)),
            dma((2,)),
            dma((4,)),
            dma((COLS,)),
            dma((COLS,)),
            dma((4,)),
            dma((4,)),
            dma((4,)),
        ],
        compiler_params=pltpu.CompilerParams(
            collective_id=0, has_side_effects=True, vmem_limit_bytes=56 * 2**20
        ),
        cost_estimate=pl.CostEstimate(
            flops=2 * 5 * B**3, bytes_accessed=24 * 2**20, transcendentals=0
        ),
    )(tab, kids, front)


def final_kernel(
    tab, part_hbm, panel_hbm, land, schur_hbm, panel_out, acc, panel, kids, f_in, p_in, k_in, f_out, p_out
):
    row = lax.axis_index("row")
    col = lax.axis_index("col")

    def fetch(k, q):
        part = pl.ds(pl.multiple_of(q * NB, NB), NB)
        return pltpu.make_async_copy(land.at[k, part], kids.at[k, part], k_in.at[k, q])

    def fetch_front(t):
        return pltpu.make_async_copy(part_hbm.at[t], acc.at[t], f_in.at[t])

    def fetch_panel(a):
        return pltpu.make_async_copy(panel_hbm.at[a], panel.at[a], p_in.at[a])

    def put_panel(a):
        return pltpu.make_async_copy(panel.at[a], panel_out.at[a], p_out.at[a])

    def put(t):
        return pltpu.make_async_copy(acc.at[t], schur_hbm.at[t], f_out.at[t])

    for a in range(4):
        fetch_panel(a).start()
        fetch_front(2 * a).start()
        fetch_front(2 * a + 1).start()

    @pl.loop(0, COLS)
    def _(k):
        extent = tab[k, col] & 1023

        @pl.loop(0, 4)
        def _(q):
            @pl.when(q * NB < extent)
            def _():
                fetch(k, q).start()

    at_row = lax.broadcasted_iota(jnp.int32, (NB, B), 0)
    at_col = lax.broadcasted_iota(jnp.int32, (NB, B), 1)

    @pl.loop(0, 8)
    def _(t):
        a = t // 2
        b = t % 2

        @pl.when(b == 0)
        def _():
            fetch_panel(a).wait()
            put_panel(a).start()

        fetch_front(t).wait()
        i = a * ROWS + row
        j = b * COLS + col
        keep = (i > 0) & (j > 0)

        @pl.loop(0, COLS)
        def _(k):
            code = tab[k, col]
            extent = code & 1023

            @pl.when((code != 0) & (((code >> 12) & 7) == t))
            def _():
                @pl.loop(0, 4)
                def _(q):
                    @pl.when(q * NB < extent)
                    def _():
                        fetch(k, q).wait()
                        part = pl.ds(pl.multiple_of(q * NB, NB), NB)
                        inside = (at_row + q * NB < extent) & (at_col < extent) & keep
                        acc[t, part, :] = acc[t, part, :] + jnp.where(
                            inside, kids[k, part, :].astype(F32), 0.0
                        )

        put(t).start()

    for a in range(4):
        put_panel(a).wait()
    for t in range(8):
        put(t).wait()


def final_call(tab, partial, panel, land):
    any_space = pl.BlockSpec(memory_space=pl.ANY)
    dma = pltpu.SemaphoreType.DMA
    return pl.pallas_call(
        final_kernel,
        out_shape=(
            jax.ShapeDtypeStruct((8, B, B), F32),
            jax.ShapeDtypeStruct((4, B, B), F32),
        ),
        in_specs=[pl.BlockSpec(memory_space=pltpu.SMEM)] + [any_space] * 3,
        out_specs=(any_space, any_space),
        scratch_shapes=[
            pltpu.VMEM((8, B, B), F32),
            pltpu.VMEM((4, B, B), F32),
            pltpu.VMEM((COLS, B, B), BF16),
            dma((8,)),
            dma((4,)),
            dma((COLS, 4)),
            dma((8,)),
            dma((4,)),
        ],
        compiler_params=pltpu.CompilerParams(vmem_limit_bytes=56 * 2**20),
        cost_estimate=pl.CostEstimate(
            flops=8 * B**2, bytes_accessed=36 * 2**20, transcendentals=0
        ),
    )(tab, partial, panel, land)


def per_device(front_init, child_tiles, child_map, child_counts, child_extent):
    row = lax.axis_index("row")
    maps = lax.dynamic_index_in_dim(child_map, row, 0, False)
    counts = lax.dynamic_index_in_dim(child_counts, row, 0, False)
    extents = lax.dynamic_index_in_dim(child_extent, row, 0, False)
    slots = jnp.arange(8, dtype=jnp.int32)[None, :]
    tile = maps[:, :, 0] // ROWS * 2 + maps[:, :, 1] // COLS
    code = (1 << 20) + slots * (1 << 16) + tile * (1 << 12) + extents
    code = jnp.where(slots < counts[:, None], code, 0)
    dests = jnp.arange(COLS, dtype=jnp.int32)[None, None, :]
    hit = (maps[:, :, 1] % COLS)[:, :, None] == dests
    tab = jnp.sum(jnp.where(hit, code[:, :, None], 0), axis=1)
    kids = child_tiles.reshape(8, B, B)
    land, panel, partial = main_call(tab, kids, front_init.reshape(4, 2, B, B))
    schur, panel = final_call(tab, partial, panel, land)
    return schur.reshape(4, 1, 2, 1, B, B), panel.reshape(4, 1, B, B)


def solution(mesh):
    in_specs = (
        P(None, "row", None, "col", None, None),
        P("row", "col", None, None, None),
        P(),
        P(),
        P(),
    )
    out_specs = (P(None, "row", None, "col", None, None), P(None, "row", None, None))
    return jax.shard_map(
        per_device, mesh=mesh, in_specs=in_specs, out_specs=out_specs, check_vma=False
    )
```

```python
import functools

import jax
import jax.numpy as jnp
from jax import lax
from jax.experimental import pallas as pl
from jax.experimental.pallas import tpu as pltpu
from jax.sharding import PartitionSpec as P

MESH = pl.DeviceIdType.MESH
HIGH = lax.Precision.HIGHEST
F32 = jnp.float32
BF16 = jnp.bfloat16
B = 512
NB = 128
SLICE = 32
COLS = 16
ROWS = 8
HOOKS = (0, 1)
BULK = ((), (), (), (1, 2, 3, 6, 7), (14, 15, 10, 11, 4, 5, 12, 13, 8, 9), (), ())


def dot_nt(a, b, precision=HIGH):
    return lax.dot_general(
        a, b, (((1,), (1,)), ((), ())), precision=precision, preferred_element_type=F32
    )


def dot_nn(a, b, precision=HIGH):
    return lax.dot_general(
        a, b, (((1,), (0,)), ((), ())), precision=precision, preferred_element_type=F32
    )


def wide(x):
    return jnp.broadcast_to(x, (8, NB))


def factor_block(s):
    lane = lax.broadcasted_iota(jnp.int32, (8, NB), 1)
    sub = lax.broadcasted_iota(jnp.int32, (8, NB), 0)
    groups = NB // 8
    rows = [s[8 * p : 8 * p + 8, :] for p in range(groups)]
    eye = [jnp.where(lane == sub + 8 * p, 1.0, 0.0).astype(F32) for p in range(groups)]
    out_u, out_v = [], []
    for p in range(groups):
        r, e = rows[p], eye[p]
        cols = [wide(r[:, 8 * p + t : 8 * p + t + 1]) for t in range(8)]
        inv = [jnp.where(sub == t, 1.0, 0.0).astype(F32) for t in range(8)]
        pivots = None
        for t in range(8):
            pivot = wide(cols[t][t : t + 1, :])
            pivots = pivot if t == 0 else jnp.where(sub == t, pivot, pivots)
            m = jnp.where(sub > t, cols[t], 0.0) * (1.0 / pivot)
            for j in range(t + 1, 8):
                cols[j] = cols[j] - m * wide(cols[j][t : t + 1, :])
            for j in range(t + 1):
                inv[j] = inv[j] - m * wide(inv[j][t : t + 1, :])
        scale = lax.rsqrt(pivots)
        u = jnp.zeros_like(r)
        v = jnp.zeros_like(e)
        for t in range(8):
            u = u + inv[t] * wide(r[t : t + 1, :])
            v = v + inv[t] * wide(e[t : t + 1, :])
        u = u * scale
        v = v * scale
        out_u.append(jnp.where(lane >= sub + 8 * p, u, 0.0))
        out_v.append(v)
        if p < groups - 1:
            ut = jnp.transpose(u)
            for q in range(p + 1, groups):
                coef = ut[8 * q : 8 * q + 8, :]
                for t in range(8):
                    c = wide(coef[:, t : t + 1])
                    rows[q] = rows[q] - c * wide(u[t : t + 1, :])
                    eye[q] = eye[q] - c * wide(v[t : t + 1, :])
    return jnp.concatenate(out_u, 0), jnp.concatenate(out_v, 0)


def factor_step(j, s, l_ref, v_ref):
    a, b = NB * j, NB * j + NB
    u, v = factor_block(s[a:b, a:b])
    l_ref[a:b, a:b] = jnp.transpose(u)
    v_ref[a:b, a:b] = v
    if j:
        w = dot_nn(l_ref[a:b, 0:a], v_ref[0:a, 0:a])
        v_ref[a:b, 0:a] = -dot_nn(v, w)
    if b < B:
        low = dot_nt(s[b:B, a:b], v)
        l_ref[b:B, a:b] = low
        s[b:B, b:B] = s[b:B, b:B] - dot_nt(low, low)


def main_kernel(
    tab,
    kids_hbm,
    front_hbm,
    land,
    panel_hbm,
    part_hbm,
    kids,
    bucket,
    land0,
    fslice,
    pivot,
    col0,
    s,
    l_ref,
    v_ref,
    panel,
    own_need,
    need,
    front,
    w_hi,
    w_lo,
    loc,
    f_in,
    f_out,
    cut_s,
    cut_r,
    fs_s,
    fs_r,
    ft_s,
    ft_r,
    pr_s,
    pr_r,
    pg_s,
    pg_r,
    px,
    lz_s,
    lz_r,
    hz_s,
    hz_r,
    gy,
    ax,
    bk_s,
    bk_r,
    nd_s,
    nd_t,
    nd_r,
):
    row = lax.axis_index("row")
    col = lax.axis_index("col")
    zy = col // 2
    core = col % 2
    z = zy // 2
    yh = zy % 2
    x = row % 4
    yl = row // 4

    def remote(src, dst, ss, rs, to):
        return pltpu.make_async_remote_copy(
            src_ref=src, dst_ref=dst, send_sem=ss, recv_sem=rs, device_id=to, device_id_type=MESH
        )

    def kin(d):
        z = lax.rem(zy // 2 + d // 2, 4)
        return z * 2 + lax.rem(zy + d, 2)

    def mate(d):
        return kin(d // 2) * 2 + lax.rem(core + d, 2)

    def fellow(d):
        x = lax.rem(row + d, 4)
        return lax.rem(row // 4 + d // 4, 2) * 4 + x

    sibling = (row, zy * 2 + 1 - core)

    load = pltpu.make_async_copy(kids_hbm, kids, loc.at[0])
    load.start()

    barrier = pltpu.get_barrier_semaphore()

    @pl.loop(1, COLS)
    def _(d):
        pl.semaphore_signal(barrier, inc=1, device_id=(row, mate(d)), device_id_type=MESH)

    @pl.loop(1, ROWS)
    def _(d):
        pl.semaphore_signal(barrier, inc=1, device_id=(fellow(d), col), device_id_type=MESH)

    pl.semaphore_wait(barrier, COLS - 1 + ROWS - 1)

    def first_part(k):
        return front_hbm.at[0, 0, pl.ds(pl.multiple_of(k * SLICE, SLICE), SLICE), :]

    def rest_part(k):
        return front_hbm.at[1:4, 0, pl.ds(pl.multiple_of(k * SLICE, SLICE), SLICE), :]

    def first_cut(d):
        k = mate(d)
        return remote(first_part(k), fslice.at[0], fs_s.at[d], fs_r, (row, k))

    def rest_cut(d):
        k = mate(d)
        return remote(rest_part(k), fslice.at[1:4], ft_s.at[d], ft_r, (row, k))

    first_own = pltpu.make_async_copy(first_part(col), fslice.at[0], loc.at[1])
    rest_own = pltpu.make_async_copy(rest_part(col), fslice.at[1:4], loc.at[4])

    @pl.when(col == 0)
    def _():
        first_own.start()

        @pl.loop(1, COLS)
        def _(d):
            first_cut(d).start()

    load.wait()

    def pack(k):
        slot = (tab[col, k] >> 16) & 7

        @pl.loop(0, 4)
        def _(q):
            part = pl.ds(pl.multiple_of(q * NB, NB), NB)
            bucket[k, part, :] = kids[slot, part, :]

    pack(0)

    def cut(d):
        k = mate(d)
        return remote(
            bucket.at[0, pl.ds(pl.multiple_of(k * SLICE, SLICE), SLICE), :],
            land0.at[col],
            cut_s.at[d],
            cut_r.at[col],
            (row, k),
        )

    def cut_from(d):
        k = mate(d)
        return remote(bucket.at[0, 0:SLICE, :], land0.at[k], cut_s.at[d], cut_r.at[k], (row, k))

    @pl.loop(1, COLS)
    def _(d):
        cut(d).start()

    def bulk(d):
        k = mate(d)
        return remote(bucket.at[k], land.at[col], bk_s.at[d], bk_r.at[col], (row, k))

    def bulk_from(d):
        k = mate(d)
        return remote(bucket.at[k], land.at[k], bk_s.at[d], bk_r.at[k], (row, k))

    keep_own = pltpu.make_async_copy(bucket.at[col], land.at[col], loc.at[2])

    def start_bulk(stage):
        for d in BULK[stage]:
            bulk(d).start()

    land0[col] = bucket[0, pl.ds(pl.multiple_of(col * SLICE, SLICE), SLICE), :]

    @pl.loop(1, COLS)
    def _(k):
        pack(k)

    keep_own.start()

    @pl.when(col == 0)
    def _():
        rest_own.start()

        @pl.loop(1, COLS)
        def _(d):
            rest_cut(d).start()

    def fetch(t):
        return pltpu.make_async_copy(front_hbm.at[t // 2, t % 2], front.at[t], f_in.at[t])

    for t in range(8):
        fetch(t).start()

    start_bulk(0)

    @pl.loop(1, COLS)
    def _(d):
        cut_from(d).wait_recv()

    @pl.when(col == 0)
    def _():
        first_own.wait()

    @pl.when(col != 0)
    def _():
        first_cut(1).wait_recv()

    at_row = col * SLICE + lax.broadcasted_iota(jnp.int32, (SLICE, B), 0)
    at_col = lax.broadcasted_iota(jnp.int32, (SLICE, B), 1)

    def add_kids(tiles):
        @pl.loop(0, COLS)
        def _(k):
            code = tab[k, 0]
            extent = code & 1023
            tile = (code >> 12) & 7
            inside = (at_row < extent) & (at_col < extent)
            part = jnp.where(inside, land0[k].astype(F32), 0.0)
            for a in tiles:
                fslice[a] = fslice[a] + jnp.where(tile == 2 * a, part, 0.0)

    add_kids((0,))

    def pivot_row(d):
        here = pivot.at[zy, core]
        return remote(here, here, pr_s.at[d], pr_r, (fellow(d), col))

    @pl.when(row == 0)
    def _():
        pivot[zy, core] = fslice[0]

        @pl.loop(1, ROWS)
        def _(d):
            pivot_row(d).start()

    @pl.when(row != 0)
    def _():
        pivot_row(1).wait_recv()

    def pivot_col(d, there):
        here = pivot.at[there, core]
        return remote(here, here, pg_s.at[d], pg_r.at[there], (row, kin(d) * 2 + core))

    @pl.loop(1, ROWS)
    def _(d):
        pivot_col(d, zy).start()

    start_bulk(1)

    @pl.when(col == 0)
    def _():
        rest_own.wait()

    @pl.when(col != 0)
    def _():
        rest_cut(1).wait_recv()

    add_kids((1, 2, 3))

    for a in range(4):
        col0[a, z, yh, core] = fslice[a]

    partner = (row, z * 4 + (1 - yh) * 2 + core)

    def along(d):
        return (row, lax.rem(z + d, 4) * 4 + yh * 2 + core)

    def low_z(d, there):
        here = col0.at[0:2, there, yh, core]
        return remote(here, here, lz_s.at[d], lz_r.at[there], along(d))

    def low_y(side):
        here = col0.at[0:2, :, side, core]
        return remote(here, here, gy.at[0], gy.at[1], partner)

    def high_y(side):
        here = col0.at[2:4, z, side, core]
        return remote(here, here, gy.at[2], gy.at[3], partner)

    def high_z(d, there):
        here = col0.at[2:4, there, :, core]
        return remote(here, here, hz_s.at[d], hz_r.at[there], along(d))

    high_y(yh).start()

    @pl.loop(1, 4)
    def _(d):
        low_z(d, z).start()

    start_bulk(2)

    @pl.loop(1, ROWS)
    def _(d):
        pivot_col(d, kin(d)).wait_recv()

    def pivot_swap(which):
        here = pivot.at[:, which]
        return remote(here, here, px.at[0], px.at[1], sibling)

    pivot_swap(core).start()

    start_bulk(3)

    pivot_swap(1 - core).wait_recv()
    for i in range(4):
        for j in range(4):
            f = pivot[2 * i : 2 * i + 2, :, :, NB * j : NB * j + NB].reshape(NB, NB)
            g = pivot[2 * j : 2 * j + 2, :, :, NB * i : NB * i + NB].reshape(NB, NB)
            s[NB * i : NB * i + NB, NB * j : NB * j + NB] = 0.5 * (f + jnp.transpose(g))
    l_ref[...] = jnp.zeros_like(l_ref)
    v_ref[...] = jnp.zeros_like(v_ref)

    def gather_swap(which):
        here = col0.at[:, :, :, which]
        return remote(here, here, ax.at[0], ax.at[1], sibling)

    def relay_cross():
        high_y(1 - yh).wait_recv()

        @pl.loop(1, 4)
        def _(d):
            high_z(d, z).start()

        @pl.loop(1, 4)
        def _(d):
            low_z(d, lax.rem(z + d, 4)).wait_recv()

        low_y(yh).start()
        start_bulk(4)

    def relay_swap():
        low_y(1 - yh).wait_recv()

        @pl.loop(1, 4)
        def _(d):
            high_z(d, lax.rem(z + d, 4)).wait_recv()

        gather_swap(core).start()
        start_bulk(5)

    hooks = {HOOKS[0]: relay_cross, HOOKS[1]: relay_swap}
    for j in range(4):
        factor_step(j, s, l_ref, v_ref)
        if j in hooks:
            hooks[j]()

    gather_swap(1 - core).wait_recv()

    for i in range(4):
        for j in range(i, 4):
            here = (slice(NB * i, NB * i + NB), slice(NB * j, NB * j + NB))
            w = jnp.transpose(v_ref[here[1], here[0]])
            hi = w.astype(BF16)
            w_hi[here] = hi
            w_lo[here] = (w - hi.astype(F32)).astype(BF16)
    for w in (w_hi, w_lo):
        w[NB : 2 * NB, 0:NB] = jnp.zeros((NB, NB), BF16)
        w[3 * NB : B, 2 * NB : 3 * NB] = jnp.zeros((NB, NB), BF16)

    half = B // 2

    root = col % ROWS

    def solve(part, put):
        hi = part.astype(BF16)
        lo = (part - hi.astype(F32)).astype(BF16)
        for c0, depth in ((0, half), (half, B)):
            wh = w_hi[0:depth, c0 : c0 + half]
            wl = w_lo[0:depth, c0 : c0 + half]
            put(
                c0,
                dot_nn(hi[:, 0:depth], wh, None)
                + dot_nn(hi[:, 0:depth], wl, None)
                + dot_nn(lo[:, 0:depth], wh, None),
            )

    def piece(ref, g):
        return ref.at[:, pl.ds(pl.multiple_of(g * NB, NB), NB), :]

    def beside(d):
        return lax.rem(x + d, 4)

    def deal(d):
        g = beside(d)
        to = (yl * 4 + g, col)
        return remote(piece(own_need, g), piece(need, g), nd_t.at[d], nd_r.at[g], to)

    def hand(d, ref, g):
        to = (yl * 4 + beside(d), col)
        return remote(piece(ref, g), piece(need, g), nd_s.at[d], nd_r.at[g], to)

    def over(ref):
        to = ((1 - yl) * 4 + x, col)
        return remote(piece(ref, x), piece(need, x), nd_s.at[0], nd_r.at[x], to)

    need_own = pltpu.make_async_copy(own_need, need, loc.at[5])

    @pl.when(row == root)
    def _():
        @pl.loop(0, 2)
        def _(b):
            def put_need(c0, value):
                for q in range(4):
                    own_need[b, c0 : c0 + half, NB * q : NB * q + NB] = jnp.transpose(
                        value[NB * q : NB * q + NB, :]
                    ).astype(BF16)

            solve(col0[col // ROWS + 2 * b].reshape(B, B), put_need)

        over(own_need).start()

        @pl.loop(1, 4)
        def _(d):
            deal(d).start()

        @pl.loop(1, 4)
        def _(d):
            hand(d, own_need, x).start()

        need_own.start()

    @pl.when((row != root) & (yl == root // 4))
    def _():
        hand(1, need, x).wait_recv()
        over(need).start()

        @pl.loop(1, 4)
        def _(d):
            @pl.when(beside(d) != root % 4)
            def _():
                hand(d, need, x).start()

    @pl.loop(0, 4)
    def _(a):
        def put_panel(c0, value):
            panel[a, :, c0 : c0 + half] = value

        solve(col0[a].reshape(B, B), put_panel)

    @pl.when(row == 0)
    def _():
        panel[0] = l_ref[...]

    panel_out = pltpu.make_async_copy(panel, panel_hbm, loc.at[3])
    panel_out.start()

    @pl.when(row == root)
    def _():
        need_own.wait()
        over(own_need).wait_send()

        @pl.loop(1, 4)
        def _(d):
            deal(d).wait_send()
            hand(d, own_need, x).wait_send()

    @pl.when((row != root) & (yl == root // 4))
    def _():
        @pl.loop(1, 4)
        def _(d):
            hand(d, need, beside(d)).wait_recv()

        over(need).wait_send()

        @pl.loop(1, 4)
        def _(d):
            @pl.when(beside(d) != root % 4)
            def _():
                hand(d, need, x).wait_send()

    @pl.when(yl != root // 4)
    def _():
        hand(1, need, x).wait_recv()

        @pl.loop(1, 4)
        def _(d):
            hand(d, need, x).start()

        @pl.loop(1, 4)
        def _(d):
            hand(d, need, beside(d)).wait_recv()

        @pl.loop(1, 4)
        def _(d):
            hand(d, need, x).wait_send()

    start_bulk(6)

    for t in range(8):
        fetch(t).wait()

    def put(t):
        return pltpu.make_async_copy(front.at[t], part_hbm.at[t], f_out.at[t])

    @pl.loop(0, 8)
    def _(t):
        a = t // 2
        b = t % 2
        keep = (a * ROWS + row > 0) & (b * COLS + col > 0)
        p = panel[a]
        hi = p.astype(BF16)
        lo = (p - hi.astype(F32)).astype(BF16)
        update = dot_nn(hi, need[b], None) + dot_nn(lo, need[b], None)
        front[t] = jnp.where(keep, front[t] - update, 0.0)
        put(t).start()

    @pl.when(row == 0)
    def _():
        @pl.loop(1, ROWS)
        def _(d):
            pivot_row(d).wait_send()

    @pl.when(col == 0)
    def _():
        @pl.loop(1, COLS)
        def _(d):
            first_cut(d).wait_send()
            rest_cut(d).wait_send()

    pivot_swap(core).wait_send()
    low_y(yh).wait_send()
    high_y(yh).wait_send()
    gather_swap(core).wait_send()

    @pl.loop(1, ROWS)
    def _(d):
        pivot_col(d, zy).wait_send()

    @pl.loop(1, 4)
    def _(d):
        low_z(d, z).wait_send()
        high_z(d, z).wait_send()

    @pl.loop(1, COLS)
    def _(d):
        cut(d).wait_send()
        bulk(d).wait_send()

    @pl.loop(1, COLS)
    def _(d):
        bulk_from(d).wait_recv()

    keep_own.wait()
    panel_out.wait()
    for t in range(8):
        put(t).wait()


def main_call(tab, kids, front):
    any_space = pl.BlockSpec(memory_space=pl.ANY)
    dma = pltpu.SemaphoreType.DMA
    return pl.pallas_call(
        main_kernel,
        out_shape=(
            jax.ShapeDtypeStruct((COLS, B, B), BF16),
            jax.ShapeDtypeStruct((4, B, B), F32),
            jax.ShapeDtypeStruct((8, B, B), F32),
        ),
        in_specs=[pl.BlockSpec(memory_space=pltpu.SMEM), any_space, any_space],
        out_specs=(any_space,) * 3,
        scratch_shapes=[
            pltpu.VMEM((8, B, B), BF16),
            pltpu.VMEM((COLS, B, B), BF16),
            pltpu.VMEM((COLS, SLICE, B), BF16),
            pltpu.VMEM((4, SLICE, B), F32),
            pltpu.VMEM((8, 2, SLICE, B), F32),
            pltpu.VMEM((4, 4, 2, 2, SLICE, B), F32),
            pltpu.VMEM((B, B), F32),
            pltpu.VMEM((B, B), F32),
            pltpu.VMEM((B, B), F32),
            pltpu.VMEM((4, B, B), F32),
            pltpu.VMEM((2, B, B), BF16),
            pltpu.VMEM((2, B, B), BF16),
            pltpu.VMEM((8, B, B), F32),
            pltpu.VMEM((B, B), BF16),
            pltpu.VMEM((B, B), BF16),
            dma((6,)),
            dma((8,)),
            dma((8,)),
            dma((COLS,)),
            dma((COLS,)),
            dma((COLS,)),
            dma,
            dma((COLS,)),
            dma,
            dma((ROWS,)),
            dma,
            dma((ROWS,)),
            dma((ROWS,)),
            dma((2,)),
            dma((4,)),
            dma((4,)),
            dma((4,)),
            dma((4,)),
            dma((4,)),
            dma((2,)),
            dma((COLS,)),
            dma((COLS,)),
            dma((4,)),
            dma((4,)),
            dma((4,)),
        ],
        compiler_params=pltpu.CompilerParams(
            collective_id=0, has_side_effects=True, vmem_limit_bytes=56 * 2**20
        ),
        cost_estimate=pl.CostEstimate(
            flops=2 * 5 * B**3, bytes_accessed=24 * 2**20, transcendentals=0
        ),
    )(tab, kids, front)


def final_kernel(
    tab, part_hbm, panel_hbm, land, schur_hbm, panel_out, acc, panel, kids, f_in, p_in, k_in, f_out, p_out
):
    row = lax.axis_index("row")
    col = lax.axis_index("col")

    def fetch(k, q):
        part = pl.ds(pl.multiple_of(q * NB, NB), NB)
        return pltpu.make_async_copy(land.at[k, part], kids.at[k, part], k_in.at[k, q])

    def fetch_front(t):
        return pltpu.make_async_copy(part_hbm.at[t], acc.at[t], f_in.at[t])

    def fetch_panel(a):
        return pltpu.make_async_copy(panel_hbm.at[a], panel.at[a], p_in.at[a])

    def put_panel(a):
        return pltpu.make_async_copy(panel.at[a], panel_out.at[a], p_out.at[a])

    def put(t):
        return pltpu.make_async_copy(acc.at[t], schur_hbm.at[t], f_out.at[t])

    for a in range(4):
        fetch_panel(a).start()
        fetch_front(2 * a).start()
        fetch_front(2 * a + 1).start()

    @pl.loop(0, COLS)
    def _(k):
        extent = tab[k, col] & 1023

        @pl.loop(0, 4)
        def _(q):
            @pl.when(q * NB < extent)
            def _():
                fetch(k, q).start()

    at_row = lax.broadcasted_iota(jnp.int32, (NB, B), 0)
    at_col = lax.broadcasted_iota(jnp.int32, (NB, B), 1)

    @pl.loop(0, 8)
    def _(t):
        a = t // 2
        b = t % 2

        @pl.when(b == 0)
        def _():
            fetch_panel(a).wait()
            put_panel(a).start()

        fetch_front(t).wait()
        i = a * ROWS + row
        j = b * COLS + col
        keep = (i > 0) & (j > 0)

        @pl.loop(0, COLS)
        def _(k):
            code = tab[k, col]
            extent = code & 1023

            @pl.when((code != 0) & (((code >> 12) & 7) == t))
            def _():
                @pl.loop(0, 4)
                def _(q):
                    @pl.when(q * NB < extent)
                    def _():
                        fetch(k, q).wait()
                        part = pl.ds(pl.multiple_of(q * NB, NB), NB)
                        inside = (at_row + q * NB < extent) & (at_col < extent) & keep
                        acc[t, part, :] = acc[t, part, :] + jnp.where(
                            inside, kids[k, part, :].astype(F32), 0.0
                        )

        put(t).start()

    for a in range(4):
        put_panel(a).wait()
    for t in range(8):
        put(t).wait()


def final_call(tab, partial, panel, land):
    any_space = pl.BlockSpec(memory_space=pl.ANY)
    dma = pltpu.SemaphoreType.DMA
    return pl.pallas_call(
        final_kernel,
        out_shape=(
            jax.ShapeDtypeStruct((8, B, B), F32),
            jax.ShapeDtypeStruct((4, B, B), F32),
        ),
        in_specs=[pl.BlockSpec(memory_space=pltpu.SMEM)] + [any_space] * 3,
        out_specs=(any_space, any_space),
        scratch_shapes=[
            pltpu.VMEM((8, B, B), F32),
            pltpu.VMEM((4, B, B), F32),
            pltpu.VMEM((COLS, B, B), BF16),
            dma((8,)),
            dma((4,)),
            dma((COLS, 4)),
            dma((8,)),
            dma((4,)),
        ],
        compiler_params=pltpu.CompilerParams(vmem_limit_bytes=56 * 2**20),
        cost_estimate=pl.CostEstimate(
            flops=8 * B**2, bytes_accessed=36 * 2**20, transcendentals=0
        ),
    )(tab, partial, panel, land)


def per_device(front_init, child_tiles, child_map, child_counts, child_extent):
    row = lax.axis_index("row")
    maps = lax.dynamic_index_in_dim(child_map, row, 0, False)
    counts = lax.dynamic_index_in_dim(child_counts, row, 0, False)
    extents = lax.dynamic_index_in_dim(child_extent, row, 0, False)
    slots = jnp.arange(8, dtype=jnp.int32)[None, :]
    tile = maps[:, :, 0] // ROWS * 2 + maps[:, :, 1] // COLS
    code = (1 << 20) + slots * (1 << 16) + tile * (1 << 12) + extents
    code = jnp.where(slots < counts[:, None], code, 0)
    dests = jnp.arange(COLS, dtype=jnp.int32)[None, None, :]
    hit = (maps[:, :, 1] % COLS)[:, :, None] == dests
    tab = jnp.sum(jnp.where(hit, code[:, :, None], 0), axis=1)
    kids = child_tiles.reshape(8, B, B)
    land, panel, partial = main_call(tab, kids, front_init.reshape(4, 2, B, B))
    schur, panel = final_call(tab, partial, panel, land)
    return schur.reshape(4, 1, 2, 1, B, B), panel.reshape(4, 1, B, B)


def solution(mesh):
    in_specs = (
        P(None, "row", None, "col", None, None),
        P("row", "col", None, None, None),
        P(),
        P(),
        P(),
    )
    out_specs = (P(None, "row", None, "col", None, None), P(None, "row", None, None))
    return jax.shard_map(
        per_device, mesh=mesh, in_specs=in_specs, out_specs=out_specs, check_vma=False
    )
```

```python
import functools

import jax
import jax.numpy as jnp
from jax import lax
from jax.experimental import pallas as pl
from jax.experimental.pallas import tpu as pltpu
from jax.sharding import PartitionSpec as P

MESH = pl.DeviceIdType.MESH
HIGH = lax.Precision.HIGHEST
F32 = jnp.float32
BF16 = jnp.bfloat16
B = 512
NB = 128
SLICE = 32
COLS = 16
ROWS = 8
HOOK = 1
BULK = ((), (), (), (), (1, 2, 3, 4, 5), (12, 13, 8, 9), (6, 7, 14, 15, 10, 11))


def dot_nt(a, b, precision=HIGH):
    return lax.dot_general(
        a, b, (((1,), (1,)), ((), ())), precision=precision, preferred_element_type=F32
    )


def dot_nn(a, b, precision=HIGH):
    return lax.dot_general(
        a, b, (((1,), (0,)), ((), ())), precision=precision, preferred_element_type=F32
    )


def wide(x):
    return jnp.broadcast_to(x, (8, NB))


def factor_block(s):
    lane = lax.broadcasted_iota(jnp.int32, (8, NB), 1)
    sub = lax.broadcasted_iota(jnp.int32, (8, NB), 0)
    groups = NB // 8
    rows = [s[8 * p : 8 * p + 8, :] for p in range(groups)]
    eye = [jnp.where(lane == sub + 8 * p, 1.0, 0.0).astype(F32) for p in range(groups)]
    out_u, out_v = [], []
    for p in range(groups):
        r, e = rows[p], eye[p]
        cols = [wide(r[:, 8 * p + t : 8 * p + t + 1]) for t in range(8)]
        inv = [jnp.where(sub == t, 1.0, 0.0).astype(F32) for t in range(8)]
        pivots = None
        for t in range(8):
            pivot = wide(cols[t][t : t + 1, :])
            pivots = pivot if t == 0 else jnp.where(sub == t, pivot, pivots)
            m = jnp.where(sub > t, cols[t], 0.0) * (1.0 / pivot)
            for j in range(t + 1, 8):
                cols[j] = cols[j] - m * wide(cols[j][t : t + 1, :])
            for j in range(t + 1):
                inv[j] = inv[j] - m * wide(inv[j][t : t + 1, :])
        scale = lax.rsqrt(pivots)
        u = jnp.zeros_like(r)
        v = jnp.zeros_like(e)
        for t in range(8):
            u = u + inv[t] * wide(r[t : t + 1, :])
            v = v + inv[t] * wide(e[t : t + 1, :])
        u = u * scale
        v = v * scale
        out_u.append(jnp.where(lane >= sub + 8 * p, u, 0.0))
        out_v.append(v)
        if p < groups - 1:
            ut = jnp.transpose(u)
            for q in range(p + 1, groups):
                coef = ut[8 * q : 8 * q + 8, :]
                for t in range(8):
                    c = wide(coef[:, t : t + 1])
                    rows[q] = rows[q] - c * wide(u[t : t + 1, :])
                    eye[q] = eye[q] - c * wide(v[t : t + 1, :])
    return jnp.concatenate(out_u, 0), jnp.concatenate(out_v, 0)


def factor_step(j, s, l_ref, v_ref):
    a, b = NB * j, NB * j + NB
    u, v = factor_block(s[a:b, a:b])
    l_ref[a:b, a:b] = jnp.transpose(u)
    v_ref[a:b, a:b] = v
    if j:
        w = dot_nn(l_ref[a:b, 0:a], v_ref[0:a, 0:a])
        v_ref[a:b, 0:a] = -dot_nn(v, w)
    if b < B:
        low = dot_nt(s[b:B, a:b], v)
        l_ref[b:B, a:b] = low
        s[b:B, b:B] = s[b:B, b:B] - dot_nt(low, low)


def main_kernel(
    tab,
    kids_hbm,
    front_hbm,
    land,
    panel_hbm,
    part_hbm,
    kids,
    bucket,
    land0,
    fslice,
    pivot,
    col0,
    s,
    l_ref,
    v_ref,
    panel,
    own_need,
    need,
    front,
    w_hi,
    w_lo,
    loc,
    f_in,
    f_out,
    cut_s,
    cut_r,
    fs_s,
    fs_r,
    ft_s,
    ft_r,
    pr_s,
    pr_r,
    pg_s,
    pg_r,
    px,
    lz_s,
    lz_r,
    hz_s,
    hz_r,
    gy,
    ax,
    bk_s,
    bk_r,
    nd_s,
    nd_t,
    nd_r,
):
    row = lax.axis_index("row")
    col = lax.axis_index("col")
    zy = col // 2
    core = col % 2
    z = zy // 2
    yh = zy % 2
    x = row % 4
    yl = row // 4

    def remote(src, dst, ss, rs, to):
        return pltpu.make_async_remote_copy(
            src_ref=src, dst_ref=dst, send_sem=ss, recv_sem=rs, device_id=to, device_id_type=MESH
        )

    def kin(d):
        z = lax.rem(zy // 2 + d // 2, 4)
        return z * 2 + lax.rem(zy + d, 2)

    def mate(d):
        return kin(d // 2) * 2 + lax.rem(core + d, 2)

    def fellow(d):
        x = lax.rem(row + d, 4)
        return lax.rem(row // 4 + d // 4, 2) * 4 + x

    sibling = (row, zy * 2 + 1 - core)

    load = pltpu.make_async_copy(kids_hbm, kids, loc.at[0])
    load.start()

    barrier = pltpu.get_barrier_semaphore()

    @pl.loop(1, COLS)
    def _(d):
        pl.semaphore_signal(barrier, inc=1, device_id=(row, mate(d)), device_id_type=MESH)

    @pl.loop(1, ROWS)
    def _(d):
        pl.semaphore_signal(barrier, inc=1, device_id=(fellow(d), col), device_id_type=MESH)

    pl.semaphore_wait(barrier, COLS - 1 + ROWS - 1)

    def first_part(k):
        return front_hbm.at[0, 0, pl.ds(pl.multiple_of(k * SLICE, SLICE), SLICE), :]

    def rest_part(k):
        return front_hbm.at[1:4, 0, pl.ds(pl.multiple_of(k * SLICE, SLICE), SLICE), :]

    def first_cut(d):
        k = mate(d)
        return remote(first_part(k), fslice.at[0], fs_s.at[d], fs_r, (row, k))

    def rest_cut(d):
        k = mate(d)
        return remote(rest_part(k), fslice.at[1:4], ft_s.at[d], ft_r, (row, k))

    first_own = pltpu.make_async_copy(first_part(col), fslice.at[0], loc.at[1])
    rest_own = pltpu.make_async_copy(rest_part(col), fslice.at[1:4], loc.at[4])

    @pl.when(col == 0)
    def _():
        first_own.start()

        @pl.loop(1, COLS)
        def _(d):
            first_cut(d).start()

    load.wait()

    def pack(k):
        slot = (tab[col, k] >> 16) & 7

        @pl.loop(0, 4)
        def _(q):
            part = pl.ds(pl.multiple_of(q * NB, NB), NB)
            bucket[k, part, :] = kids[slot, part, :]

    pack(0)

    def cut(d):
        k = mate(d)
        return remote(
            bucket.at[0, pl.ds(pl.multiple_of(k * SLICE, SLICE), SLICE), :],
            land0.at[col],
            cut_s.at[d],
            cut_r.at[col],
            (row, k),
        )

    def cut_from(d):
        k = mate(d)
        return remote(bucket.at[0, 0:SLICE, :], land0.at[k], cut_s.at[d], cut_r.at[k], (row, k))

    @pl.loop(1, COLS)
    def _(d):
        cut(d).start()

    def bulk(d):
        k = mate(d)
        return remote(bucket.at[k], land.at[col], bk_s.at[d], bk_r.at[col], (row, k))

    def bulk_from(d):
        k = mate(d)
        return remote(bucket.at[k], land.at[k], bk_s.at[d], bk_r.at[k], (row, k))

    keep_own = pltpu.make_async_copy(bucket.at[col], land.at[col], loc.at[2])

    def start_bulk(stage):
        for d in BULK[stage]:
            bulk(d).start()

    land0[col] = bucket[0, pl.ds(pl.multiple_of(col * SLICE, SLICE), SLICE), :]

    @pl.loop(1, COLS)
    def _(k):
        pack(k)

    keep_own.start()

    @pl.when(col == 0)
    def _():
        rest_own.start()

        @pl.loop(1, COLS)
        def _(d):
            rest_cut(d).start()

    def fetch(t):
        return pltpu.make_async_copy(front_hbm.at[t // 2, t % 2], front.at[t], f_in.at[t])

    for t in range(8):
        fetch(t).start()

    start_bulk(0)

    @pl.loop(1, COLS)
    def _(d):
        cut_from(d).wait_recv()

    @pl.when(col == 0)
    def _():
        first_own.wait()

    @pl.when(col != 0)
    def _():
        first_cut(1).wait_recv()

    at_row = col * SLICE + lax.broadcasted_iota(jnp.int32, (SLICE, B), 0)
    at_col = lax.broadcasted_iota(jnp.int32, (SLICE, B), 1)

    def add_kids(tiles):
        @pl.loop(0, COLS)
        def _(k):
            code = tab[k, 0]
            extent = code & 1023
            tile = (code >> 12) & 7
            inside = (at_row < extent) & (at_col < extent)
            part = jnp.where(inside, land0[k].astype(F32), 0.0)
            for a in tiles:
                fslice[a] = fslice[a] + jnp.where(tile == 2 * a, part, 0.0)

    add_kids((0,))

    def pivot_row(d):
        here = pivot.at[zy, core]
        return remote(here, here, pr_s.at[d], pr_r, (fellow(d), col))

    @pl.when(row == 0)
    def _():
        pivot[zy, core] = fslice[0]

        @pl.loop(1, ROWS)
        def _(d):
            pivot_row(d).start()

    @pl.when(row != 0)
    def _():
        pivot_row(1).wait_recv()

    def pivot_col(d, there):
        here = pivot.at[there, core]
        return remote(here, here, pg_s.at[d], pg_r.at[there], (row, kin(d) * 2 + core))

    @pl.loop(1, ROWS)
    def _(d):
        pivot_col(d, zy).start()

    start_bulk(1)

    @pl.when(col == 0)
    def _():
        rest_own.wait()

    @pl.when(col != 0)
    def _():
        rest_cut(1).wait_recv()

    add_kids((1, 2, 3))

    for a in range(4):
        col0[a, z, yh, core] = fslice[a]

    partner = (row, z * 4 + (1 - yh) * 2 + core)

    def along(d):
        return (row, lax.rem(z + d, 4) * 4 + yh * 2 + core)

    def low_z(d, there):
        here = col0.at[0:2, there, yh, core]
        return remote(here, here, lz_s.at[d], lz_r.at[there], along(d))

    def low_y(side):
        here = col0.at[0:2, :, side, core]
        return remote(here, here, gy.at[0], gy.at[1], partner)

    def high_y(side):
        here = col0.at[2:4, z, side, core]
        return remote(here, here, gy.at[2], gy.at[3], partner)

    def high_z(d, there):
        here = col0.at[2:4, there, :, core]
        return remote(here, here, hz_s.at[d], hz_r.at[there], along(d))

    high_y(yh).start()

    @pl.loop(1, 4)
    def _(d):
        low_z(d, z).start()

    start_bulk(2)

    @pl.loop(1, ROWS)
    def _(d):
        pivot_col(d, kin(d)).wait_recv()

    def pivot_swap(which):
        here = pivot.at[:, which]
        return remote(here, here, px.at[0], px.at[1], sibling)

    pivot_swap(core).start()

    def gather_swap(which):
        here = col0.at[:, :, :, which]
        return remote(here, here, ax.at[0], ax.at[1], sibling)

    def relay_cross():
        high_y(1 - yh).wait_recv()

        @pl.loop(1, 4)
        def _(d):
            high_z(d, z).start()

        @pl.loop(1, 4)
        def _(d):
            low_z(d, lax.rem(z + d, 4)).wait_recv()

        low_y(yh).start()
        start_bulk(4)

    def relay_swap():
        low_y(1 - yh).wait_recv()

        @pl.loop(1, 4)
        def _(d):
            high_z(d, lax.rem(z + d, 4)).wait_recv()

        gather_swap(core).start()
        start_bulk(5)

    relay_cross()

    pivot_swap(1 - core).wait_recv()
    for i in range(4):
        for j in range(4):
            f = pivot[2 * i : 2 * i + 2, :, :, NB * j : NB * j + NB].reshape(NB, NB)
            g = pivot[2 * j : 2 * j + 2, :, :, NB * i : NB * i + NB].reshape(NB, NB)
            s[NB * i : NB * i + NB, NB * j : NB * j + NB] = 0.5 * (f + jnp.transpose(g))
    l_ref[...] = jnp.zeros_like(l_ref)
    v_ref[...] = jnp.zeros_like(v_ref)

    hooks = {HOOK: relay_swap}
    for j in range(4):
        factor_step(j, s, l_ref, v_ref)
        if j in hooks:
            hooks[j]()

    gather_swap(1 - core).wait_recv()

    for i in range(4):
        for j in range(i, 4):
            here = (slice(NB * i, NB * i + NB), slice(NB * j, NB * j + NB))
            w = jnp.transpose(v_ref[here[1], here[0]])
            hi = w.astype(BF16)
            w_hi[here] = hi
            w_lo[here] = (w - hi.astype(F32)).astype(BF16)
    for w in (w_hi, w_lo):
        w[NB : 2 * NB, 0:NB] = jnp.zeros((NB, NB), BF16)
        w[3 * NB : B, 2 * NB : 3 * NB] = jnp.zeros((NB, NB), BF16)

    half = B // 2

    root = col % ROWS

    def solve(part, put):
        hi = part.astype(BF16)
        lo = (part - hi.astype(F32)).astype(BF16)
        for c0, depth in ((0, half), (half, B)):
            wh = w_hi[0:depth, c0 : c0 + half]
            wl = w_lo[0:depth, c0 : c0 + half]
            put(
                c0,
                dot_nn(hi[:, 0:depth], wh, None)
                + dot_nn(hi[:, 0:depth], wl, None)
                + dot_nn(lo[:, 0:depth], wh, None),
            )

    def piece(ref, g):
        return ref.at[:, pl.ds(pl.multiple_of(g * NB, NB), NB), :]

    def beside(d):
        return lax.rem(x + d, 4)

    def deal(d):
        g = beside(d)
        to = (yl * 4 + g, col)
        return remote(piece(own_need, g), piece(need, g), nd_t.at[d], nd_r.at[g], to)

    def hand(d, ref, g):
        to = (yl * 4 + beside(d), col)
        return remote(piece(ref, g), piece(need, g), nd_s.at[d], nd_r.at[g], to)

    def over(ref):
        to = ((1 - yl) * 4 + x, col)
        return remote(piece(ref, x), piece(need, x), nd_s.at[0], nd_r.at[x], to)

    need_own = pltpu.make_async_copy(own_need, need, loc.at[5])

    @pl.when(row == root)
    def _():
        @pl.loop(0, 2)
        def _(b):
            def put_need(c0, value):
                for q in range(4):
                    own_need[b, c0 : c0 + half, NB * q : NB * q + NB] = jnp.transpose(
                        value[NB * q : NB * q + NB, :]
                    ).astype(BF16)

            solve(col0[col // ROWS + 2 * b].reshape(B, B), put_need)

        over(own_need).start()

        @pl.loop(1, 4)
        def _(d):
            deal(d).start()

        @pl.loop(1, 4)
        def _(d):
            hand(d, own_need, x).start()

        need_own.start()
        start_bulk(6)

    @pl.when((row != root) & (yl == root // 4))
    def _():
        hand(1, need, x).wait_recv()
        over(need).start()

        @pl.loop(1, 4)
        def _(d):
            @pl.when(beside(d) != root % 4)
            def _():
                hand(d, need, x).start()

        start_bulk(6)

    @pl.loop(0, 4)
    def _(a):
        def put_panel(c0, value):
            panel[a, :, c0 : c0 + half] = value

        solve(col0[a].reshape(B, B), put_panel)

    @pl.when(row == 0)
    def _():
        panel[0] = l_ref[...]

    panel_out = pltpu.make_async_copy(panel, panel_hbm, loc.at[3])
    panel_out.start()

    @pl.when(row == root)
    def _():
        need_own.wait()
        over(own_need).wait_send()

        @pl.loop(1, 4)
        def _(d):
            deal(d).wait_send()
            hand(d, own_need, x).wait_send()

    @pl.when((row != root) & (yl == root // 4))
    def _():
        @pl.loop(1, 4)
        def _(d):
            hand(d, need, beside(d)).wait_recv()

        over(need).wait_send()

        @pl.loop(1, 4)
        def _(d):
            @pl.when(beside(d) != root % 4)
            def _():
                hand(d, need, x).wait_send()

    @pl.when(yl != root // 4)
    def _():
        hand(1, need, x).wait_recv()

        @pl.loop(1, 4)
        def _(d):
            hand(d, need, x).start()

        start_bulk(6)

        @pl.loop(1, 4)
        def _(d):
            hand(d, need, beside(d)).wait_recv()

        @pl.loop(1, 4)
        def _(d):
            hand(d, need, x).wait_send()

    for t in range(8):
        fetch(t).wait()

    def put(t):
        return pltpu.make_async_copy(front.at[t], part_hbm.at[t], f_out.at[t])

    @pl.loop(0, 8)
    def _(t):
        a = t // 2
        b = t % 2
        keep = (a * ROWS + row > 0) & (b * COLS + col > 0)
        p = panel[a]
        hi = p.astype(BF16)
        lo = (p - hi.astype(F32)).astype(BF16)
        update = dot_nn(hi, need[b], None) + dot_nn(lo, need[b], None)
        front[t] = jnp.where(keep, front[t] - update, 0.0)
        put(t).start()

    @pl.when(row == 0)
    def _():
        @pl.loop(1, ROWS)
        def _(d):
            pivot_row(d).wait_send()

    @pl.when(col == 0)
    def _():
        @pl.loop(1, COLS)
        def _(d):
            first_cut(d).wait_send()
            rest_cut(d).wait_send()

    pivot_swap(core).wait_send()
    low_y(yh).wait_send()
    high_y(yh).wait_send()
    gather_swap(core).wait_send()

    @pl.loop(1, ROWS)
    def _(d):
        pivot_col(d, zy).wait_send()

    @pl.loop(1, 4)
    def _(d):
        low_z(d, z).wait_send()
        high_z(d, z).wait_send()

    @pl.loop(1, COLS)
    def _(d):
        cut(d).wait_send()
        bulk(d).wait_send()

    @pl.loop(1, COLS)
    def _(d):
        bulk_from(d).wait_recv()

    keep_own.wait()
    panel_out.wait()
    for t in range(8):
        put(t).wait()


def main_call(tab, kids, front):
    any_space = pl.BlockSpec(memory_space=pl.ANY)
    dma = pltpu.SemaphoreType.DMA
    return pl.pallas_call(
        main_kernel,
        out_shape=(
            jax.ShapeDtypeStruct((COLS, B, B), BF16),
            jax.ShapeDtypeStruct((4, B, B), F32),
            jax.ShapeDtypeStruct((8, B, B), F32),
        ),
        in_specs=[pl.BlockSpec(memory_space=pltpu.SMEM), any_space, any_space],
        out_specs=(any_space,) * 3,
        scratch_shapes=[
            pltpu.VMEM((8, B, B), BF16),
            pltpu.VMEM((COLS, B, B), BF16),
            pltpu.VMEM((COLS, SLICE, B), BF16),
            pltpu.VMEM((4, SLICE, B), F32),
            pltpu.VMEM((8, 2, SLICE, B), F32),
            pltpu.VMEM((4, 4, 2, 2, SLICE, B), F32),
            pltpu.VMEM((B, B), F32),
            pltpu.VMEM((B, B), F32),
            pltpu.VMEM((B, B), F32),
            pltpu.VMEM((4, B, B), F32),
            pltpu.VMEM((2, B, B), BF16),
            pltpu.VMEM((2, B, B), BF16),
            pltpu.VMEM((8, B, B), F32),
            pltpu.VMEM((B, B), BF16),
            pltpu.VMEM((B, B), BF16),
            dma((6,)),
            dma((8,)),
            dma((8,)),
            dma((COLS,)),
            dma((COLS,)),
            dma((COLS,)),
            dma,
            dma((COLS,)),
            dma,
            dma((ROWS,)),
            dma,
            dma((ROWS,)),
            dma((ROWS,)),
            dma((2,)),
            dma((4,)),
            dma((4,)),
            dma((4,)),
            dma((4,)),
            dma((4,)),
            dma((2,)),
            dma((COLS,)),
            dma((COLS,)),
            dma((4,)),
            dma((4,)),
            dma((4,)),
        ],
        compiler_params=pltpu.CompilerParams(
            collective_id=0, has_side_effects=True, vmem_limit_bytes=56 * 2**20
        ),
        cost_estimate=pl.CostEstimate(
            flops=2 * 5 * B**3, bytes_accessed=24 * 2**20, transcendentals=0
        ),
    )(tab, kids, front)


def final_kernel(
    tab, part_hbm, panel_hbm, land, schur_hbm, panel_out, acc, panel, kids, f_in, p_in, k_in, f_out, p_out
):
    row = lax.axis_index("row")
    col = lax.axis_index("col")

    def fetch(k, q):
        part = pl.ds(pl.multiple_of(q * NB, NB), NB)
        return pltpu.make_async_copy(land.at[k, part], kids.at[k, part], k_in.at[k, q])

    def fetch_front(t):
        return pltpu.make_async_copy(part_hbm.at[t], acc.at[t], f_in.at[t])

    def fetch_panel(a):
        return pltpu.make_async_copy(panel_hbm.at[a], panel.at[a], p_in.at[a])

    def put_panel(a):
        return pltpu.make_async_copy(panel.at[a], panel_out.at[a], p_out.at[a])

    def put(t):
        return pltpu.make_async_copy(acc.at[t], schur_hbm.at[t], f_out.at[t])

    for a in range(4):
        fetch_panel(a).start()
        fetch_front(2 * a).start()
        fetch_front(2 * a + 1).start()

    @pl.loop(0, COLS)
    def _(k):
        extent = tab[k, col] & 1023

        @pl.loop(0, 4)
        def _(q):
            @pl.when(q * NB < extent)
            def _():
                fetch(k, q).start()

    at_row = lax.broadcasted_iota(jnp.int32, (NB, B), 0)
    at_col = lax.broadcasted_iota(jnp.int32, (NB, B), 1)

    @pl.loop(0, 8)
    def _(t):
        a = t // 2
        b = t % 2

        @pl.when(b == 0)
        def _():
            fetch_panel(a).wait()
            put_panel(a).start()

        fetch_front(t).wait()
        i = a * ROWS + row
        j = b * COLS + col
        keep = (i > 0) & (j > 0)

        @pl.loop(0, COLS)
        def _(k):
            code = tab[k, col]
            extent = code & 1023

            @pl.when((code != 0) & (((code >> 12) & 7) == t))
            def _():
                @pl.loop(0, 4)
                def _(q):
                    @pl.when(q * NB < extent)
                    def _():
                        fetch(k, q).wait()
                        part = pl.ds(pl.multiple_of(q * NB, NB), NB)
                        inside = (at_row + q * NB < extent) & (at_col < extent) & keep
                        acc[t, part, :] = acc[t, part, :] + jnp.where(
                            inside, kids[k, part, :].astype(F32), 0.0
                        )

        put(t).start()

    for a in range(4):
        put_panel(a).wait()
    for t in range(8):
        put(t).wait()


def final_call(tab, partial, panel, land):
    any_space = pl.BlockSpec(memory_space=pl.ANY)
    dma = pltpu.SemaphoreType.DMA
    return pl.pallas_call(
        final_kernel,
        out_shape=(
            jax.ShapeDtypeStruct((8, B, B), F32),
            jax.ShapeDtypeStruct((4, B, B), F32),
        ),
        in_specs=[pl.BlockSpec(memory_space=pltpu.SMEM)] + [any_space] * 3,
        out_specs=(any_space, any_space),
        scratch_shapes=[
            pltpu.VMEM((8, B, B), F32),
            pltpu.VMEM((4, B, B), F32),
            pltpu.VMEM((COLS, B, B), BF16),
            dma((8,)),
            dma((4,)),
            dma((COLS, 4)),
            dma((8,)),
            dma((4,)),
        ],
        compiler_params=pltpu.CompilerParams(vmem_limit_bytes=56 * 2**20),
        cost_estimate=pl.CostEstimate(
            flops=8 * B**2, bytes_accessed=36 * 2**20, transcendentals=0
        ),
    )(tab, partial, panel, land)


def per_device(front_init, child_tiles, child_map, child_counts, child_extent):
    row = lax.axis_index("row")
    maps = lax.dynamic_index_in_dim(child_map, row, 0, False)
    counts = lax.dynamic_index_in_dim(child_counts, row, 0, False)
    extents = lax.dynamic_index_in_dim(child_extent, row, 0, False)
    slots = jnp.arange(8, dtype=jnp.int32)[None, :]
    tile = maps[:, :, 0] // ROWS * 2 + maps[:, :, 1] // COLS
    code = (1 << 20) + slots * (1 << 16) + tile * (1 << 12) + extents
    code = jnp.where(slots < counts[:, None], code, 0)
    dests = jnp.arange(COLS, dtype=jnp.int32)[None, None, :]
    hit = (maps[:, :, 1] % COLS)[:, :, None] == dests
    tab = jnp.sum(jnp.where(hit, code[:, :, None], 0), axis=1)
    kids = child_tiles.reshape(8, B, B)
    land, panel, partial = main_call(tab, kids, front_init.reshape(4, 2, B, B))
    schur, panel = final_call(tab, partial, panel, land)
    return schur.reshape(4, 1, 2, 1, B, B), panel.reshape(4, 1, B, B)


def solution(mesh):
    in_specs = (
        P(None, "row", None, "col", None, None),
        P("row", "col", None, None, None),
        P(),
        P(),
        P(),
    )
    out_specs = (P(None, "row", None, "col", None, None), P(None, "row", None, None))
    return jax.shard_map(
        per_device, mesh=mesh, in_specs=in_specs, out_specs=out_specs, check_vma=False
    )
```
